32 devices in a mesh: parts: 2 (over y), tensor: 16 (over z, x, core).
Axes of the slice: x: 2, y: 2, z: 4, core: 2. Of those that a mesh axis runs over, the one named last changes fastest.
Arguments:
- tokens: bfloat16 [32, 8192], P(('parts', 'tensor')), parts along dimension 0, may hold values from -6 to 6
- cotangent: bfloat16 [32, 8192], P(('parts', 'tensor')), parts along dimension 0, may hold values from -6 to 6
- token_adapter_index: int32 [32], P(('parts', 'tensor')), parts along dimension 0, may hold values from 0 to 63
- adapter_storage_slot: int32 [64], replicated, may hold values from 0 to 63, each once
- gate_weight: bfloat16 [8192, 16384], P(None, 'tensor'), may hold values from -0.0625 to 0.0625
- up_weight: bfloat16 [8192, 16384], P(None, 'tensor'), may hold values from -0.0625 to 0.0625
- down_weight: bfloat16 [16384, 8192], P('tensor'), may hold values from -0.046875 to 0.046875
- adapter_down_factors: bfloat16 [64, 16, 16384], P(None, None, 'tensor'), may hold values from -0.046875 to 0.046875
- adapter_up_factors: bfloat16 [64, 16, 8192], P('tensor'), may hold values from -1.5 to 1.5
Outputs:
- mixed: bfloat16 [32, 8192], P(('parts', 'tensor')), parts along dimension 0
- input_grad: bfloat16 [32, 8192], P(('parts', 'tensor')), parts along dimension 0
- down_grad: bfloat16 [128, 16, 16384], P('parts', None, 'tensor'), parts along dimension 0
- up_factor_gradient: bfloat16 [128, 16, 8192], P(('parts', 'tensor')), parts along dimension 0
The draws below stay inside these ranges and needn't reach their ends.
There are 2 independent parts, one for each index of `parts`. The reference program is written for one: setup_inputs(seed, part) draws one part's arguments, and reference() takes and returns one part's arrays. A program takes and returns all parts, laid end to end along the dimension named above; an argument that names none is the same for every part. Nothing has to cross between parts.
Inputs may be any that keep to these rules, and one draw needn't show every extreme that they name: `adapter_storage_slot`: each slot once.
All inputs are finite; a program needn't handle non-finite values.
Results may differ from the reference program's by a relative error of at most 0.009.
Values may be sent and summed in bfloat16 or wider, within the bound.
No kernel may reach another device: no remote copies, remote signals or barrier semaphores. Data moves between devices by JAX's collectives and lax.ppermute only.
A program may use at most 128 MiB of HBM per device.

```python
import math
import jax
import jax.numpy as jnp
import numpy as np

MODEL_WIDTH = 8192
HIDDEN_UNITS = 16384
ADAPTER_RANK = 16
ADAPTER_COUNT = 64
TOKENS = 16


def touch_ends(array, own_key, smallest, high):
    dims = array.shape
    spot = [jax.random.randint(jax.random.fold_in(own_key, axis), (), 0, dims[axis]) for axis in range(len(dims))]
    array = array.at[tuple(spot)].set(smallest)
    longest = dims.index(max(dims))
    spot[longest] = (spot[longest] + 1) % dims[longest]
    return array.at[tuple(spot)].set(high)


def steps_of(rng, dims, pieces, smallest, high):
    factor_of, own = 1.0, jax.random.fold_in(rng, 6)
    for axis_at, shards_of in pieces:
        heights = jnp.exp(jax.random.uniform(jax.random.fold_in(own, axis_at), (shards_of,), jnp.float32, smallest / len(pieces), high / len(pieces)))
        factor_of = factor_of * jnp.repeat(heights, dims[axis_at] // shards_of).reshape([-1 if axis == axis_at else 1 for axis in range(len(dims))])
    return factor_of


def rank_bounds(number_of, lean):
    portions = [(1 << 20) // math.isqrt(standing ** lean) + 1 for standing in range(1, number_of + 1)]
    scale = 1 + sum(portions) // (1 << 30)
    return np.cumsum(np.array([max(1, weight // scale) for weight in portions]))


def ranked_ids(stream_key, dims, amount, slope):
    listing = rank_bounds(amount, slope)
    pick = jax.random.randint(jax.random.fold_in(stream_key, 1), dims, 0, int(listing[amount - 1]))
    rank = jnp.searchsorted(jnp.asarray(listing, jnp.int32), pick, side="right")
    return jax.random.permutation(jax.random.fold_in(stream_key, 2), amount)[rank].astype(jnp.int32)


def scatter_about(stream_key, dims, deviation, reach, pieces=(), kind=jnp.bfloat16):
    values = jax.random.normal(stream_key, dims, jnp.float32) * deviation
    if len(pieces) > 0:
        values = steps_of(stream_key, dims, pieces, -0.22, 0.18) * values
    return jnp.clip(values, min=-reach, max=reach).astype(kind)


def setup_inputs(seed: int = 0, part: int = 0) -> dict:
    keys = jax.random.split(jax.random.key(seed), 10)
    part_keys = jax.random.split(jax.random.fold_in(keys[9], part), 10)
    return {
        "tokens": scatter_about(part_keys[0], (TOKENS, MODEL_WIDTH), 1.0, 6.0, ((0, 16),)),
        "cotangent": scatter_about(part_keys[1], (TOKENS, MODEL_WIDTH), 1.0, 6.0, ((0, 16),)),
        "token_adapter_index": touch_ends(ranked_ids(part_keys[2], (TOKENS,), ADAPTER_COUNT, 2), jax.random.fold_in(part_keys[2], 3), 0, ADAPTER_COUNT - 1).astype(jnp.int32),
        "adapter_storage_slot": jax.random.permutation(keys[3], ADAPTER_COUNT).astype(jnp.int32),
        "gate_weight": scatter_about(keys[4], (MODEL_WIDTH, HIDDEN_UNITS), MODEL_WIDTH ** -0.5, 0.0625, ((1, 16),)),
        "up_weight": scatter_about(keys[5], (MODEL_WIDTH, HIDDEN_UNITS), MODEL_WIDTH ** -0.5, 0.0625, ((1, 16),)),
        "down_weight": scatter_about(keys[6], (HIDDEN_UNITS, MODEL_WIDTH), HIDDEN_UNITS ** -0.5, 0.046875, ((0, 16),)),
        "adapter_down_factors": scatter_about(keys[7], (ADAPTER_COUNT, ADAPTER_RANK, HIDDEN_UNITS), HIDDEN_UNITS ** -0.5, 0.046875, ((2, 16),)),
        "adapter_up_factors": scatter_about(keys[8], (ADAPTER_COUNT, ADAPTER_RANK, MODEL_WIDTH), ADAPTER_RANK ** -0.5, 1.5, ((0, 16),)),
    }


adapter_scale = 2.0


def reference(tokens, cotangent, token_adapter_index, adapter_storage_slot, gate_weight, up_weight, down_weight, adapter_down_factors, adapter_up_factors):
    storage_position = adapter_storage_slot[token_adapter_index].astype(jnp.int32)
    gate = jnp.dot(tokens, gate_weight, preferred_element_type=jnp.float32)
    up = jnp.dot(tokens, up_weight, preferred_element_type=jnp.float32)
    sig = jax.nn.sigmoid(gate)
    silu = gate * sig
    hidden_units_value = (silu * up).astype(jnp.bfloat16)
    down_factor_rows = adapter_down_factors[storage_position].astype(jnp.float32)
    up_factor_rows = adapter_up_factors[storage_position].astype(jnp.float32)
    rank_input = jnp.einsum('lb,lsb->ls', hidden_units_value.astype(jnp.float32), down_factor_rows)
    adapted_output = (adapter_scale * jnp.einsum('of,ofu->ou', rank_input, up_factor_rows)).astype(jnp.bfloat16)
    mixed = (jnp.dot(hidden_units_value, down_weight, preferred_element_type=jnp.float32) + adapted_output.astype(jnp.float32)).astype(jnp.bfloat16)
    output_cotangent = cotangent.astype(jnp.float32)
    rank_output = (adapter_scale * jnp.einsum('wo,wmo->wm', output_cotangent, up_factor_rows)).astype(jnp.bfloat16)
    hidden_gradient = jnp.dot(cotangent, down_weight.T, preferred_element_type=jnp.float32)
    hidden_gradient = hidden_gradient + jnp.einsum('nz,nzu->nu', rank_output.astype(jnp.float32), down_factor_rows)
    gate_grad = (hidden_gradient * up * sig * (1.0 + gate * (1.0 - sig))).astype(jnp.bfloat16)
    up_grad_h = (hidden_gradient * silu).astype(jnp.bfloat16)
    input_grad = (jnp.dot(gate_grad, gate_weight.T, preferred_element_type=jnp.float32) + jnp.dot(up_grad_h, up_weight.T, preferred_element_type=jnp.float32)).astype(jnp.bfloat16)
    count = adapter_storage_slot.shape[0]
    down_terms = rank_output.astype(jnp.float32)[:, :, None] * hidden_units_value.astype(jnp.float32)[:, None, :]
    down_grad = jax.ops.segment_sum(down_terms, storage_position, num_segments=count).astype(jnp.bfloat16)
    up_factor_pieces = adapter_scale * rank_input[:, :, None] * output_cotangent[:, None, :]
    up_factor_gradient = jax.ops.segment_sum(up_factor_pieces, storage_position, num_segments=count).astype(jnp.bfloat16)
    return mixed, input_grad, down_grad, up_factor_gradient
```

```python
import functools

import jax
import jax.numpy as jnp
from jax import lax
from jax.experimental import pallas as pl
from jax.experimental.pallas import tpu as pltpu
from jax.sharding import PartitionSpec as P

adapter_scale = 2.0
f32 = jnp.float32
bf16 = jnp.bfloat16
SPLIT = 128
VMEM = pl.BlockSpec(memory_space=pltpu.VMEM)
NT = (((1,), (1,)), ((), ()))
TN = (((0,), (0,)), ((), ()))


def params(mib):
    return pltpu.CompilerParams(vmem_limit_bytes=mib << 20)


def fit(size, want):
    return want if size % want == 0 else size


def slot_mask(slot, first, columns, rank):
    col = lax.broadcasted_iota(jnp.int32, (slot.shape[0], columns), 1) // rank
    return slot.astype(jnp.int32) == col + first


def fold_matrix(columns, rank, by_row):
    shape = (columns, rank) if by_row else (rank, columns)
    c = lax.broadcasted_iota(jnp.int32, shape, 0 if by_row else 1)
    r = lax.broadcasted_iota(jnp.int32, shape, 1 if by_row else 0)
    return jnp.where(c % rank == r, 1.0, 0.0).astype(bf16)


def halves(v):
    high = v.astype(bf16)
    return high, (v - high.astype(f32)).astype(bf16)


def dot(a, b, dims=(((1,), (0,)), ((), ()))):
    return lax.dot_general(a, b, dims, preferred_element_type=f32)


def dot2(v, b, dims=(((1,), (0,)), ((), ()))):
    high, low = halves(v)
    return dot(high, b, dims) + dot(low, b, dims)


def forward_kernel(
    x_ref, c_ref, slot_ref, wg_ref, wu_ref, d_ref, u_ref, gate_ref, up_ref, hid_ref, pay_ref
):
    total, width = x_ref.shape
    hidden_dev = wg_ref.shape[1]
    chunk = fit(width, 2048)
    half = total // 2

    def body(i, acc):
        s = pl.ds(pl.multiple_of(i * chunk, chunk), chunk)
        xs = x_ref[:, s]
        return acc[0] + dot(xs, wg_ref[s, :]), acc[1] + dot(xs, wu_ref[s, :])

    zero = jnp.zeros((total, hidden_dev), f32)
    gate, up = lax.fori_loop(0, width // chunk, body, (zero, zero))
    gate_ref[...] = gate
    up_ref[...] = up
    hid = (gate * jax.nn.sigmoid(gate) * up).astype(bf16)
    hid_ref[...] = hid
    rank = pay_ref.shape[1] // 4
    slot = slot_ref[...]
    columns = d_ref.shape[0]
    met = dot(hid, d_ref[...], NT)
    met = jnp.where(slot_mask(slot, 0, columns, rank), met, 0.0)
    rank_in = dot2(met, fold_matrix(columns, rank, True))
    kept = u_ref.shape[0]
    first = lax.axis_index("tensor") * (kept // rank)
    pulled = dot(c_ref[...], u_ref[...], NT)
    pulled = jnp.where(slot_mask(slot, first, kept, rank), pulled, 0.0)
    rank_out = adapter_scale * dot2(pulled, fold_matrix(kept, rank, True))
    both = jnp.concatenate((rank_in, rank_out), axis=1)
    swap = lax.axis_index("tensor") % 2
    own, sib = both[:half], both[half:]
    pay_ref[...] = jnp.concatenate(
        (jnp.where(swap == 0, own, sib), jnp.where(swap == 0, sib, own)), axis=1
    )


def down_kernel(hid_ref, c_ref, wd_ref, base_ref, pull_ref):
    width = wd_ref.shape[1]
    hidden_dev = wd_ref.shape[0]
    chunk = fit(width, 1024)

    def body(i, _):
        s = pl.ds(pl.multiple_of(i * chunk, chunk), chunk)
        base_ref[:, s] = dot(hid_ref[...], wd_ref[:, s])
        return 0

    lax.fori_loop(0, width // chunk, body, 0)
    rows = fit(hidden_dev, 256)

    def body2(i, _):
        s = pl.ds(pl.multiple_of(i * rows, rows), rows)
        pull_ref[:, s] = dot(c_ref[...], wd_ref[s, :], NT)
        return 0

    lax.fori_loop(0, hidden_dev // rows, body2, 0)


def backward_kernel(
    got_ref, slot_ref, gate_ref, up_ref, base_ref, pull_ref, wg_ref, wu_ref, d_ref, u_ref,
    own_ref, sib_ref, left_ref, weighted_ref,
):
    total, hidden_dev = gate_ref.shape
    width = wg_ref.shape[0]
    half = total // 2
    rank = got_ref.shape[2] // 4
    columns = d_ref.shape[0]
    kept = u_ref.shape[0]
    got = jnp.sum(got_ref[...], axis=0)
    swap = lax.axis_index("tensor") % 2
    a, b = got[:, : 2 * rank], got[:, 2 * rank :]
    both = jnp.concatenate(
        (jnp.where(swap == 0, a, b), jnp.where(swap == 0, b, a)), axis=0
    )
    rank_in = both[:, :rank]
    rank_out = both[:, rank:].astype(bf16)
    slot = slot_ref[...]
    spread = dot(rank_out, fold_matrix(columns, rank, False))
    left = jnp.where(slot_mask(slot, 0, columns, rank), spread, 0.0).astype(bf16)
    left_ref[...] = left
    grad = pull_ref[...] + dot(left, d_ref[...])
    gate = gate_ref[...]
    up = up_ref[...]
    sig = jax.nn.sigmoid(gate)
    gg = (grad * up * sig * (1.0 + gate * (1.0 - sig))).astype(bf16)
    gu = (grad * (gate * sig)).astype(bf16)
    first = lax.axis_index("tensor") * (kept // rank)
    mine = slot_mask(slot, first, kept, rank)
    high, low = halves(rank_in)
    fold = fold_matrix(kept, rank, False)
    high = jnp.where(mine, dot(high, fold), 0.0).astype(bf16)
    low = jnp.where(mine, dot(low, fold), 0.0).astype(bf16)
    weighted = jnp.concatenate((high, low), axis=0)
    weighted_ref[...] = weighted
    chunk = fit(width, 1024)

    def body(i, _):
        s = pl.ds(pl.multiple_of(i * chunk, chunk), chunk)
        us = u_ref[:, s]
        adapted = adapter_scale * (dot(high, us) + dot(low, us))
        out = base_ref[:, s] + adapted.astype(bf16).astype(f32)
        inp = dot(gg, wg_ref[s, :], NT) + dot(gu, wu_ref[s, :], NT)
        own_ref[0, :, s] = out[:half]
        own_ref[1, :, s] = inp[:half]
        sib_ref[0, :, s] = out[half:].astype(bf16)
        sib_ref[1, :, s] = inp[half:].astype(bf16)
        return 0

    lax.fori_loop(0, width // chunk, body, 0)


def factor_kernel(left_ref, hid_ref, weighted_ref, c_ref, down_ref, upg_ref):
    columns = down_ref.shape[0]
    rows = fit(columns, 256)
    for i in range(columns // rows):
        s = pl.ds(i * rows, rows)
        down_ref[s, :] = dot(left_ref[:, s], hid_ref[...], TN).astype(bf16)
    width = c_ref.shape[1]
    chunk = fit(width, 1024)
    total = c_ref.shape[0]
    for i in range(width // chunk):
        s = pl.ds(i * chunk, chunk)
        cs = c_ref[:, s]
        both = dot(weighted_ref[:total], cs, TN) + dot(weighted_ref[total:], cs, TN)
        upg_ref[:, s] = (adapter_scale * both).astype(bf16)


def call(kernel, args, outs, mib, flops=0, nbytes=0):
    return pl.pallas_call(
        kernel,
        in_specs=[VMEM] * len(args),
        out_specs=[VMEM] * len(outs),
        out_shape=[jax.ShapeDtypeStruct(s, t) for s, t in outs],
        compiler_params=params(mib),
        cost_estimate=pl.CostEstimate(flops=flops, bytes_accessed=nbytes, transcendentals=0),
    )(*args)


def per_device(
    tokens,
    cotangent,
    token_adapter_index,
    adapter_storage_slot,
    gate_weight,
    up_weight,
    down_weight,
    adapter_down_factors,
    adapter_up_factors,
):
    devices = lax.axis_size("tensor")
    chips = devices // 2
    tok_dev, width = tokens.shape
    hidden_dev = gate_weight.shape[1]
    kept, rank = adapter_up_factors.shape[:2]
    count = adapter_storage_slot.shape[0]
    half = chips * tok_dev
    total = 2 * half
    room = 8 + total // 4
    same_core = [[c + 2 * i for i in range(chips)] for c in range(2)]
    pairs = [(i, i ^ 1) for i in range(devices)]

    wg, wu, wd = (
        pltpu.with_memory_space_constraint(w, pltpu.VMEM)
        for w in (gate_weight, up_weight, down_weight)
    )
    d = pltpu.with_memory_space_constraint(
        adapter_down_factors.reshape(count * rank, hidden_dev), pltpu.VMEM
    )
    u = pltpu.with_memory_space_constraint(
        adapter_up_factors.reshape(kept * rank, width), pltpu.VMEM
    )

    table = jnp.arange(count, dtype=jnp.int32)
    slot = jnp.sum(
        jnp.where(token_adapter_index[:, None] == table[None, :], adapter_storage_slot[None, :], 0),
        axis=1,
    )
    lanes = jnp.arange(SPLIT, dtype=jnp.int32)[None, :]
    digits = jnp.where(
        lanes == 0, slot[:, None] // SPLIT, jnp.where(lanes == 1, slot[:, None] % SPLIT, 0)
    ).astype(bf16)
    row = jnp.stack(
        (
            jnp.concatenate((tokens, digits), axis=1),
            jnp.concatenate((cotangent, jnp.zeros_like(digits)), axis=1),
        ),
        axis=1,
    )
    sent = jnp.broadcast_to(row[None], (chips,) + row.shape)
    own = lax.all_to_all(sent, "tensor", 0, 0, axis_index_groups=same_core, tiled=True)
    sib = lax.ppermute(own, "tensor", pairs)
    gathered = jnp.concatenate((own, sib), axis=0).reshape(total, 2, width + SPLIT)
    x = gathered[:, 0, :width]
    c = gathered[:, 1, :width]
    code = gathered[:, 0, width : width + 2].astype(f32)
    slots = code[:, 0:1] * SPLIT + code[:, 1:2]

    gate, up, hid, pay = call(
        forward_kernel,
        (x, c, slots, wg, wu, d, u),
        (
            ((total, hidden_dev), f32),
            ((total, hidden_dev), f32),
            ((total, hidden_dev), bf16),
            ((half, 4 * rank), f32),
        ),
        room,
    )
    got = lax.all_to_all(
        jnp.broadcast_to(pay[None], (devices,) + pay.shape), "tensor", 0, 0, tiled=True
    )
    base, pull = call(
        down_kernel,
        (hid, c, wd),
        (((total, width), f32), ((total, hidden_dev), f32)),
        room,
        flops=4 * total * width * hidden_dev,
        nbytes=2 * width * hidden_dev,
    )
    mine, theirs, left, weighted = call(
        backward_kernel,
        (got, slots, gate, up, base, pull, wg, wu, d, u),
        (
            ((2, half, width), f32),
            ((2, half, width), bf16),
            ((total, count * rank), bf16),
            ((2 * total, kept * rank), bf16),
        ),
        room,
    )
    summed = mine + lax.ppermute(theirs, "tensor", pairs).astype(f32)
    summed = jnp.transpose(
        summed.astype(bf16).reshape(2, chips, tok_dev, width), (1, 0, 2, 3)
    ).reshape(chips, 2 * tok_dev, width)
    back = lax.all_to_all(summed, "tensor", 0, 0, axis_index_groups=same_core, tiled=True)
    down_grad, up_factor_gradient = call(
        factor_kernel,
        (left, hid, weighted, c),
        (((count * rank, hidden_dev), bf16), ((kept * rank, width), bf16)),
        room,
        flops=2 * total * count * rank * hidden_dev,
        nbytes=2 * (count * rank * hidden_dev + kept * rank * width),
    )
    final = jnp.sum(back.astype(f32).reshape(chips, 2, tok_dev, width), axis=0).astype(bf16)
    return (
        final[0],
        final[1],
        down_grad.reshape(count, rank, hidden_dev),
        up_factor_gradient.reshape(kept, rank, width),
    )


def solution(mesh):
    in_specs = (
        P(("parts", "tensor"), None),
        P(("parts", "tensor"), None),
        P(("parts", "tensor")),
        P(),
        P(None, "tensor"),
        P(None, "tensor"),
        P("tensor", None),
        P(None, None, "tensor"),
        P("tensor", None, None),
    )
    out_specs = (
        P(("parts", "tensor"), None),
        P(("parts", "tensor"), None),
        P("parts", None, "tensor"),
        P(("parts", "tensor"), None, None),
    )
    return jax.shard_map(
        per_device, mesh=mesh, in_specs=in_specs, out_specs=out_specs, check_vma=False
    )
```

```python
import functools

import jax
import jax.numpy as jnp
from jax import lax
from jax.experimental import pallas as pl
from jax.experimental.pallas import tpu as pltpu
from jax.sharding import PartitionSpec as P

adapter_scale = 2.0
f32 = jnp.float32
bf16 = jnp.bfloat16
AHEAD = 5
PARTS = 2
PIECE = 1 << 20
SPLIT = 128
VMEM = pl.BlockSpec(memory_space=pltpu.VMEM)
SMEM = pl.BlockSpec(memory_space=pltpu.SMEM)
HBM = pl.BlockSpec(memory_space=pltpu.HBM)
NT = (((1,), (1,)), ((), ()))
TN = (((0,), (0,)), ((), ()))


def params(mib):
    return pltpu.CompilerParams(vmem_limit_bytes=mib << 20)


def fit(size, want):
    return want if size % want == 0 else size


def slot_mask(slot, first, columns, rank):
    col = lax.broadcasted_iota(jnp.int32, (slot.shape[0], columns), 1) // rank
    return slot.astype(jnp.int32) == col + first


def fold_matrix(columns, rank, by_row):
    shape = (columns, rank) if by_row else (rank, columns)
    c = lax.broadcasted_iota(jnp.int32, shape, 0 if by_row else 1)
    r = lax.broadcasted_iota(jnp.int32, shape, 1 if by_row else 0)
    return jnp.where(c % rank == r, 1.0, 0.0).astype(bf16)


def halves(v):
    high = v.astype(bf16)
    return high, (v - high.astype(f32)).astype(bf16)


def dot(a, b, dims=(((1,), (0,)), ((), ()))):
    return lax.dot_general(a, b, dims, preferred_element_type=f32)


def dot2(v, b, dims=(((1,), (0,)), ((), ()))):
    high, low = halves(v)
    return dot(high, b, dims) + dot(low, b, dims)


class Stream:
    def __init__(self, ahead):
        self.moves, self.ahead, self.taken, self.begun = [], ahead, 0, 0

    def add(self, src, dst, sem):
        self.moves.append(pltpu.make_async_copy(src, dst, sem))

    def fill(self):
        while self.begun < min(self.taken + self.ahead, len(self.moves)):
            self.moves[self.begun].start()
            self.begun += 1

    def take(self, count=1):
        for _ in range(count):
            self.fill()
            self.moves[self.taken].wait()
            self.taken += 1
        self.fill()


def pack_kernel(
    index_ref, table_hbm, tokens_hbm, cotangent_hbm, out_ref,
    table_ref, tokens_ref, cotangent_ref, sems,
):
    moves = [
        pltpu.make_async_copy(a, b, sems.at[i])
        for i, (a, b) in enumerate(
            (
                (table_hbm, table_ref),
                (tokens_hbm, tokens_ref),
                (cotangent_hbm, cotangent_ref),
            )
        )
    ]
    for m in moves:
        m.start()
    for m in moves:
        m.wait()
    width = tokens_ref.shape[1]
    slot = table_ref[index_ref[0]]
    lane = lax.broadcasted_iota(jnp.int32, (1, SPLIT), 1)
    digits = jnp.where(lane == 0, slot // SPLIT, jnp.where(lane == 1, slot % SPLIT, 0))
    digits = digits.astype(f32).astype(bf16)
    for i in range(out_ref.shape[0]):
        out_ref[i, 0:1, :width] = tokens_ref[...]
        out_ref[i, 1:2, :width] = cotangent_ref[...]
        out_ref[i, 0:1, width:] = digits
        out_ref[i, 1:2, width:] = digits


def blocks(size, step):
    return [pl.ds(i * step, step) for i in range(size // step)]


def forward_kernel(
    rank, parts,
    x_ref, c_ref, slot_ref, wg_hbm, wu_hbm, wd_hbm, d_hbm, u_hbm,
    gate_ref, up_ref, hid_ref, pay_ref, base_ref, pull_ref, wg_ref, d_ref, u_ref,
    wu_ref, wd_ref, sg, su, sd, sf,
):
    total, width = x_ref.shape
    hidden_dev = wg_ref.shape[1]
    units = hidden_dev // parts
    tall = fit(width, PIECE // units)
    flat = fit(units, PIECE // width)
    stream = Stream(AHEAD)
    stream.add(u_hbm, u_ref, sf.at[0])
    for p, f in enumerate(blocks(hidden_dev, units)):
        for j, k in enumerate(blocks(width, tall)):
            stream.add(wg_hbm.at[k, f], wg_ref.at[k, f], sg.at[p, j])
        for j, k in enumerate(blocks(width, tall)):
            stream.add(wu_hbm.at[k, f], wu_ref.at[k], su.at[p, j])
        if p == parts - 1:
            stream.add(d_hbm, d_ref, sf.at[1])
        for j, k in enumerate(blocks(units, flat)):
            at = pl.ds(p * units + j * flat, flat)
            stream.add(wd_hbm.at[at], wd_ref.at[k], sd.at[p, j])
    stream.fill()
    half = total // 2
    slot = slot_ref[...]

    stream.take()
    kept = u_ref.shape[0]
    first = lax.axis_index("tensor") * (kept // rank)
    pulled = dot(c_ref[...], u_ref[...], NT)
    pulled = jnp.where(slot_mask(slot, first, kept, rank), pulled, 0.0)
    rank_out = adapter_scale * dot2(pulled, fold_matrix(kept, rank, True))

    def project(w_ref, f):
        acc = jnp.zeros((total, units), f32)
        for k in blocks(width, tall):
            stream.take()
            acc = acc + dot(x_ref[:, k], w_ref[k, f])
        return acc

    step = fit(width, 2048)
    for p, f in enumerate(blocks(hidden_dev, units)):
        gate = project(wg_ref, f)
        gate_ref[:, f] = gate
        up = project(wu_ref, slice(None))
        up_ref[:, f] = up
        hid = (gate * jax.nn.sigmoid(gate) * up).astype(bf16)
        hid_ref[:, f] = hid
        if p == parts - 1:
            stream.take()
            columns = d_ref.shape[0]
            met = dot(hid_ref[...], d_ref[...], NT)
            met = jnp.where(slot_mask(slot, 0, columns, rank), met, 0.0)
            rank_in = dot2(met, fold_matrix(columns, rank, True))
        for j, k in enumerate(blocks(units, flat)):
            stream.take()
            at = pl.ds(p * units + j * flat, flat)
            pull_ref[:, at] = dot(c_ref[...], wd_ref[k], NT)
        for s in blocks(width, step):
            part = dot(hid, wd_ref[:, s])
            base_ref[:, s] = part if p == 0 else base_ref[:, s] + part

    both = jnp.concatenate((rank_in, rank_out), axis=1)
    swap = lax.axis_index("tensor") % 2
    own, sib = both[:half], both[half:]
    pay = jnp.concatenate(
        (
            jnp.where(swap == 0, own, sib),
            jnp.where(swap == 0, sib, own),
            jnp.zeros((half, pay_ref.shape[2] - 4 * rank), f32),
        ),
        axis=1,
    )
    for i in range(pay_ref.shape[0]):
        pay_ref[i] = pay


def backward_kernel(
    rank,
    got_ref, slot_ref, gate_ref, up_ref, base_ref, pull_ref, wg_ref, wu_hbm, d_ref, u_ref,
    own_ref, sib_ref, left_ref, weighted_ref,
    wu_ref, su,
):
    total, hidden_dev = gate_ref.shape
    width = wg_ref.shape[0]
    piece = fit(width, 1024)
    stream = Stream(AHEAD)
    for j, k in enumerate(blocks(width, piece)):
        stream.add(wu_hbm.at[k], wu_ref.at[k], su.at[j])
    stream.fill()
    half = total // 2
    columns = d_ref.shape[0]
    kept = u_ref.shape[0]
    got = jnp.sum(got_ref[...], axis=0)
    swap = lax.axis_index("tensor") % 2
    a, b = got[:, : 2 * rank], got[:, 2 * rank : 4 * rank]
    both = jnp.concatenate(
        (jnp.where(swap == 0, a, b), jnp.where(swap == 0, b, a)), axis=0
    )
    rank_in = both[:, :rank]
    rank_out = both[:, rank:].astype(bf16)
    spread = dot(rank_out, fold_matrix(columns, rank, False))
    slot = slot_ref[...]
    left = jnp.where(slot_mask(slot, 0, columns, rank), spread, 0.0).astype(bf16)
    left_ref[...] = left
    grad = pull_ref[...] + dot(left, d_ref[...])
    gate = gate_ref[...]
    up = up_ref[...]
    sig = jax.nn.sigmoid(gate)
    gg = (grad * up * sig * (1.0 + gate * (1.0 - sig))).astype(bf16)
    gu = (grad * (gate * sig)).astype(bf16)
    first = lax.axis_index("tensor") * (kept // rank)
    mine = slot_mask(slot, first, kept, rank)
    high, low = halves(rank_in)
    fold = fold_matrix(kept, rank, False)
    high = jnp.where(mine, dot(high, fold), 0.0).astype(bf16)
    low = jnp.where(mine, dot(low, fold), 0.0).astype(bf16)
    weighted_ref[...] = jnp.concatenate((high, low), axis=0)
    for s in blocks(width, 2 * piece):
        us = u_ref[:, s]
        adapted = adapter_scale * (dot(high, us) + dot(low, us))
        out = base_ref[:, s] + adapted.astype(bf16).astype(f32)
        own_ref[0, :, s] = out[:half]
        sib_ref[0, :, s] = out[half:].astype(bf16)
        inp = dot(gg, wg_ref[s, :], NT)
        stream.take(2)
        inp = inp + dot(gu, wu_ref[s, :], NT)
        own_ref[1, :, s] = inp[:half]
        sib_ref[1, :, s] = inp[half:].astype(bf16)


def factor_kernel(left_ref, hid_ref, weighted_ref, c_ref, down_ref, upg_ref):
    columns = down_ref.shape[0]
    rows = fit(columns, 256)
    for i in range(columns // rows):
        s = pl.ds(i * rows, rows)
        down_ref[s, :] = dot(left_ref[:, s], hid_ref[...], TN).astype(bf16)
    width = c_ref.shape[1]
    chunk = fit(width, 1024)
    total = c_ref.shape[0]
    for i in range(width // chunk):
        s = pl.ds(i * chunk, chunk)
        cs = c_ref[:, s]
        both = dot(weighted_ref[:total], cs, TN) + dot(weighted_ref[total:], cs, TN)
        upg_ref[:, s] = (adapter_scale * both).astype(bf16)


def call(kernel, args, outs, mib, specs=None, out_specs=None, flops=0, nbytes=0, scratch=()):
    return pl.pallas_call(
        kernel,
        in_specs=specs or [VMEM] * len(args),
        out_specs=out_specs or [VMEM] * len(outs),
        out_shape=[jax.ShapeDtypeStruct(*o) if isinstance(o, tuple) else o for o in outs],
        scratch_shapes=scratch,
        compiler_params=params(mib),
        cost_estimate=pl.CostEstimate(flops=flops, bytes_accessed=nbytes, transcendentals=0),
    )(*args)


def held(x):
    return pltpu.with_memory_space_constraint(x, pltpu.VMEM)


def far(x):
    return pltpu.with_memory_space_constraint(x, pltpu.HBM)


def per_device(
    tokens,
    cotangent,
    token_adapter_index,
    adapter_storage_slot,
    gate_weight,
    up_weight,
    down_weight,
    adapter_down_factors,
    adapter_up_factors,
):
    devices = lax.axis_size("tensor")
    chips = devices // 2
    tok_dev, width = tokens.shape
    hidden_dev = gate_weight.shape[1]
    kept, rank = adapter_up_factors.shape[:2]
    count = adapter_storage_slot.shape[0]
    half = chips * tok_dev
    total = 2 * half
    room = 4 if total <= 16 else 40
    same_core = [[c + 2 * i for i in range(chips)] for c in range(2)]
    pairs = [(i, i ^ 1) for i in range(devices)]
    parts = PARTS if hidden_dev % (256 * PARTS) == 0 else 1
    units = hidden_dev // parts

    wg, wu, wd = far(gate_weight), far(up_weight), far(down_weight)
    d = far(adapter_down_factors.reshape(count * rank, hidden_dev))
    u = far(adapter_up_factors.reshape(kept * rank, width))
    weight_mib = -(-2 * width * hidden_dev >> 20)

    (sent,) = call(
        pack_kernel,
        (token_adapter_index, far(adapter_storage_slot), far(tokens), far(cotangent)),
        (((chips, 2, width + SPLIT), bf16),),
        room,
        specs=[SMEM] + [HBM] * 3,
        scratch=[
            pltpu.SMEM(adapter_storage_slot.shape, jnp.int32),
            pltpu.VMEM(tokens.shape, bf16),
            pltpu.VMEM(cotangent.shape, bf16),
            pltpu.SemaphoreType.DMA((3,)),
        ],
    )
    own = lax.all_to_all(sent, "tensor", 0, 0, axis_index_groups=same_core, tiled=True)
    sib = lax.ppermute(own, "tensor", pairs)
    gathered = jnp.concatenate((own, sib), axis=0).reshape(total, 2, width + SPLIT)
    x = gathered[:, 0, :width]
    c = gathered[:, 1, :width]
    code = gathered[:, 0, width : width + 2].astype(f32)
    slots = code[:, 0:1] * SPLIT + code[:, 1:2]

    sems = pltpu.SemaphoreType.DMA
    gate, up, hid, pay, base, pull, wg, d, u = call(
        functools.partial(forward_kernel, rank, parts),
        (x, c, slots, wg, wu, wd, d, u),
        (
            ((total, hidden_dev), f32),
            ((total, hidden_dev), f32),
            ((total, hidden_dev), bf16),
            ((devices, half, -(-4 * rank // 128) * 128), f32),
            ((total, width), f32),
            ((total, hidden_dev), f32),
            pltpu.VMEM(wg.shape, bf16),
            pltpu.VMEM(d.shape, bf16),
            pltpu.VMEM(u.shape, bf16),
        ),
        room + -(-2 * weight_mib // parts),
        specs=[VMEM] * 3 + [HBM] * 5,
        scratch=[
            pltpu.VMEM((width, units), bf16),
            pltpu.VMEM((units, width), bf16),
            sems((parts, width // fit(width, PIECE // units))),
            sems((parts, width // fit(width, PIECE // units))),
            sems((parts, units // fit(units, PIECE // width))),
            sems((2,)),
        ],
    )
    got = lax.all_to_all(pay, "tensor", 0, 0)
    mine, theirs, left, weighted = call(
        functools.partial(backward_kernel, rank),
        (got, slots, gate, up, base, pull, held(wg), wu, held(d), held(u)),
        (
            ((2, half, width), f32),
            ((2, half, width), bf16),
            ((total, count * rank), bf16),
            ((2 * total, kept * rank), bf16),
        ),
        room + 6 + weight_mib,
        specs=[VMEM] * 7 + [HBM, VMEM, VMEM],
        scratch=[pltpu.VMEM(wu.shape, bf16), sems((width // fit(width, 1024),))],
    )
    summed = mine + lax.ppermute(theirs, "tensor", pairs).astype(f32)
    summed = jnp.transpose(
        summed.astype(bf16).reshape(2, chips, tok_dev, width), (1, 0, 2, 3)
    ).reshape(chips, 2 * tok_dev, width)
    back = lax.all_to_all(summed, "tensor", 0, 0, axis_index_groups=same_core, tiled=True)
    down_grad, up_factor_gradient = call(
        factor_kernel,
        (left, hid, weighted, c),
        (((count * rank, hidden_dev), bf16), ((kept * rank, width), bf16)),
        room,
        flops=2 * total * count * rank * hidden_dev,
        nbytes=2 * (count * rank * hidden_dev + kept * rank * width),
    )
    final = jnp.sum(back.astype(f32).reshape(chips, 2, tok_dev, width), axis=0).astype(bf16)
    return (
        final[0],
        final[1],
        down_grad.reshape(count, rank, hidden_dev),
        up_factor_gradient.reshape(kept, rank, width),
    )


def solution(mesh):
    in_specs = (
        P(("parts", "tensor"), None),
        P(("parts", "tensor"), None),
        P(("parts", "tensor")),
        P(),
        P(None, "tensor"),
        P(None, "tensor"),
        P("tensor", None),
        P(None, None, "tensor"),
        P("tensor", None, None),
    )
    out_specs = (
        P(("parts", "tensor"), None),
        P(("parts", "tensor"), None),
        P("parts", None, "tensor"),
        P(("parts", "tensor"), None, None),
    )
    return jax.shard_map(
        per_device, mesh=mesh, in_specs=in_specs, out_specs=out_specs, check_vma=False
    )
```

```python
import functools

import jax
import jax.numpy as jnp
from jax import lax
from jax.experimental import pallas as pl
from jax.experimental.pallas import tpu as pltpu
from jax.sharding import PartitionSpec as P

adapter_scale = 2.0
f32 = jnp.float32
bf16 = jnp.bfloat16
AHEAD = 8
PARTS = 2
PIECE = 1 << 20
SPLIT = 128
VMEM = pl.BlockSpec(memory_space=pltpu.VMEM)
SMEM = pl.BlockSpec(memory_space=pltpu.SMEM)
HBM = pl.BlockSpec(memory_space=pltpu.HBM)
NT = (((1,), (1,)), ((), ()))
TN = (((0,), (0,)), ((), ()))


def params(mib):
    return pltpu.CompilerParams(vmem_limit_bytes=mib << 20)


def fit(size, want):
    return want if size % want == 0 else size


def slot_mask(slot, first, columns, rank):
    col = lax.broadcasted_iota(jnp.int32, (slot.shape[0], columns), 1) // rank
    return slot.astype(jnp.int32) == col + first


def fold_matrix(columns, rank, by_row):
    shape = (columns, rank) if by_row else (rank, columns)
    c = lax.broadcasted_iota(jnp.int32, shape, 0 if by_row else 1)
    r = lax.broadcasted_iota(jnp.int32, shape, 1 if by_row else 0)
    return jnp.where(c % rank == r, 1.0, 0.0).astype(bf16)


def halves(v):
    high = v.astype(bf16)
    return high, (v - high.astype(f32)).astype(bf16)


def dot(a, b, dims=(((1,), (0,)), ((), ()))):
    return lax.dot_general(a, b, dims, preferred_element_type=f32)


def dot2(v, b, dims=(((1,), (0,)), ((), ()))):
    high, low = halves(v)
    return dot(high, b, dims) + dot(low, b, dims)


class Stream:
    def __init__(self, ahead):
        self.moves, self.ahead, self.taken, self.begun = [], ahead, 0, 0

    def add(self, src, dst, sem):
        self.moves.append(pltpu.make_async_copy(src, dst, sem))

    def fill(self):
        while self.begun < min(self.taken + self.ahead, len(self.moves)):
            self.moves[self.begun].start()
            self.begun += 1

    def take(self, count=1):
        for _ in range(count):
            self.fill()
            self.moves[self.taken].wait()
            self.taken += 1
        self.fill()


def pack_kernel(
    index_ref, table_hbm, tokens_hbm, cotangent_hbm, out_ref,
    table_ref, tokens_ref, cotangent_ref, sems,
):
    moves = [
        pltpu.make_async_copy(a, b, sems.at[i])
        for i, (a, b) in enumerate(
            (
                (table_hbm, table_ref),
                (tokens_hbm, tokens_ref),
                (cotangent_hbm, cotangent_ref),
            )
        )
    ]
    for m in moves:
        m.start()
    for m in moves:
        m.wait()
    width = tokens_ref.shape[1]
    slot = table_ref[index_ref[0]]
    lane = lax.broadcasted_iota(jnp.int32, (1, SPLIT), 1)
    digits = jnp.where(lane == 0, slot // SPLIT, jnp.where(lane == 1, slot % SPLIT, 0))
    digits = digits.astype(f32).astype(bf16)
    for i in range(out_ref.shape[0]):
        out_ref[i, 0:1, :width] = tokens_ref[...]
        out_ref[i, 1:2, :width] = cotangent_ref[...]
        out_ref[i, 0:1, width:] = digits
        out_ref[i, 1:2, width:] = digits


def blocks(size, step):
    return [pl.ds(i * step, step) for i in range(size // step)]


def forward_kernel(
    rank, parts,
    x_ref, c_ref, slot_ref, wg_hbm, wu_hbm, wd_hbm, d_hbm, u_hbm,
    gate_ref, up_ref, hid_ref, pay_ref, base_ref, pull_ref, wg_ref, d_ref, u_ref,
    wu_ref, wd_ref, sg, su, sd, sf,
):
    total, width = x_ref.shape
    hidden_dev = wg_ref.shape[1]
    units = hidden_dev // parts
    tall = fit(width, PIECE // units)
    flat = fit(units, PIECE // width)
    stream = Stream(AHEAD)
    stream.add(u_hbm, u_ref, sf.at[0])
    for p, f in enumerate(blocks(hidden_dev, units)):
        for j, k in enumerate(blocks(width, tall)):
            stream.add(wg_hbm.at[k, f], wg_ref.at[k, f], sg.at[p, j])
        for j, k in enumerate(blocks(width, tall)):
            stream.add(wu_hbm.at[k, f], wu_ref.at[k], su.at[p, j])
        if p == parts - 1:
            stream.add(d_hbm, d_ref, sf.at[1])
        for j, k in enumerate(blocks(units, flat)):
            at = pl.ds(p * units + j * flat, flat)
            stream.add(wd_hbm.at[at], wd_ref.at[k], sd.at[p, j])
    stream.fill()
    half = total // 2
    slot = slot_ref[...]

    stream.take()
    kept = u_ref.shape[0]
    first = lax.axis_index("tensor") * (kept // rank)
    pulled = dot(c_ref[...], u_ref[...], NT)
    pulled = jnp.where(slot_mask(slot, first, kept, rank), pulled, 0.0)
    rank_out = adapter_scale * dot2(pulled, fold_matrix(kept, rank, True))

    def project(w_ref, f):
        acc = jnp.zeros((total, units), f32)
        for k in blocks(width, fit(width, 2 * tall)):
            stream.take(k.size // tall)
            acc = acc + dot(x_ref[:, k], w_ref[k, f])
        return acc

    step = fit(width, 2048)
    for p, f in enumerate(blocks(hidden_dev, units)):
        gate = project(wg_ref, f)
        gate_ref[:, f] = gate
        up = project(wu_ref, slice(None))
        up_ref[:, f] = up
        hid = (gate * jax.nn.sigmoid(gate) * up).astype(bf16)
        hid_ref[:, f] = hid
        if p == parts - 1:
            stream.take()
            columns = d_ref.shape[0]
            met = dot(hid_ref[...], d_ref[...], NT)
            met = jnp.where(slot_mask(slot, 0, columns, rank), met, 0.0)
            rank_in = dot2(met, fold_matrix(columns, rank, True))
        stream.take(units // flat)
        pull_ref[:, f] = dot(c_ref[...], wd_ref[...], NT)
        for s in blocks(width, step):
            part = dot(hid, wd_ref[:, s])
            base_ref[:, s] = part if p == 0 else base_ref[:, s] + part

    both = jnp.concatenate((rank_in, rank_out), axis=1)
    swap = lax.axis_index("tensor") % 2
    own, sib = both[:half], both[half:]
    pay = jnp.concatenate(
        (
            jnp.where(swap == 0, own, sib),
            jnp.where(swap == 0, sib, own),
            jnp.zeros((half, pay_ref.shape[2] - 4 * rank), f32),
        ),
        axis=1,
    )
    for i in range(pay_ref.shape[0]):
        pay_ref[i] = pay


def backward_kernel(
    rank,
    got_ref, slot_ref, gate_ref, up_ref, base_ref, pull_ref, wg_ref, wu_hbm, d_ref, u_ref,
    own_ref, sib_ref, left_ref, weighted_ref,
    wu_ref, su,
):
    total, hidden_dev = gate_ref.shape
    width = wg_ref.shape[0]
    piece = fit(width, 1024)
    stream = Stream(AHEAD)
    for j, k in enumerate(blocks(width, piece)):
        stream.add(wu_hbm.at[k], wu_ref.at[k], su.at[j])
    stream.fill()
    half = total // 2
    columns = d_ref.shape[0]
    kept = u_ref.shape[0]
    got = jnp.sum(got_ref[...], axis=0)
    swap = lax.axis_index("tensor") % 2
    a, b = got[:, : 2 * rank], got[:, 2 * rank : 4 * rank]
    both = jnp.concatenate(
        (jnp.where(swap == 0, a, b), jnp.where(swap == 0, b, a)), axis=0
    )
    rank_in = both[:, :rank]
    rank_out = both[:, rank:].astype(bf16)
    spread = dot(rank_out, fold_matrix(columns, rank, False))
    slot = slot_ref[...]
    left = jnp.where(slot_mask(slot, 0, columns, rank), spread, 0.0).astype(bf16)
    left_ref[...] = left
    grad = pull_ref[...] + dot(left, d_ref[...])
    gate = gate_ref[...]
    up = up_ref[...]
    sig = jax.nn.sigmoid(gate)
    gg = (grad * up * sig * (1.0 + gate * (1.0 - sig))).astype(bf16)
    gu = (grad * (gate * sig)).astype(bf16)
    first = lax.axis_index("tensor") * (kept // rank)
    mine = slot_mask(slot, first, kept, rank)
    high, low = halves(rank_in)
    fold = fold_matrix(kept, rank, False)
    high = jnp.where(mine, dot(high, fold), 0.0).astype(bf16)
    low = jnp.where(mine, dot(low, fold), 0.0).astype(bf16)
    weighted_ref[...] = jnp.concatenate((high, low), axis=0)
    for s in blocks(width, 2 * piece):
        us = u_ref[:, s]
        adapted = adapter_scale * (dot(high, us) + dot(low, us))
        out = base_ref[:, s] + adapted.astype(bf16).astype(f32)
        own_ref[0, :, s] = out[:half]
        sib_ref[0, :, s] = out[half:].astype(bf16)
        stream.take(2)
        for i in range(8):
            t = pl.ds(s.start + i * piece // 4, piece // 4)
            inp = dot(gg, wg_ref[t, :], NT) + dot(gu, wu_ref[t, :], NT)
            own_ref[1, :, t] = inp[:half]
            sib_ref[1, :, t] = inp[half:].astype(bf16)


def factor_kernel(left_ref, hid_ref, weighted_ref, c_ref, down_ref, upg_ref):
    columns = down_ref.shape[0]
    rows = fit(columns, 256)
    for i in range(columns // rows):
        s = pl.ds(i * rows, rows)
        down_ref[s, :] = dot(left_ref[:, s], hid_ref[...], TN).astype(bf16)
    width = c_ref.shape[1]
    chunk = fit(width, 1024)
    total = c_ref.shape[0]
    for i in range(width // chunk):
        s = pl.ds(i * chunk, chunk)
        cs = c_ref[:, s]
        both = dot(weighted_ref[:total], cs, TN) + dot(weighted_ref[total:], cs, TN)
        upg_ref[:, s] = (adapter_scale * both).astype(bf16)


def call(kernel, args, outs, mib, specs=None, out_specs=None, flops=0, nbytes=0, scratch=()):
    return pl.pallas_call(
        kernel,
        in_specs=specs or [VMEM] * len(args),
        out_specs=out_specs or [VMEM] * len(outs),
        out_shape=[jax.ShapeDtypeStruct(*o) if isinstance(o, tuple) else o for o in outs],
        scratch_shapes=scratch,
        compiler_params=params(mib),
        cost_estimate=pl.CostEstimate(flops=flops, bytes_accessed=nbytes, transcendentals=0),
    )(*args)


def held(x):
    return pltpu.with_memory_space_constraint(x, pltpu.VMEM)


def far(x):
    return pltpu.with_memory_space_constraint(x, pltpu.HBM)


def per_device(
    tokens,
    cotangent,
    token_adapter_index,
    adapter_storage_slot,
    gate_weight,
    up_weight,
    down_weight,
    adapter_down_factors,
    adapter_up_factors,
):
    devices = lax.axis_size("tensor")
    chips = devices // 2
    tok_dev, width = tokens.shape
    hidden_dev = gate_weight.shape[1]
    kept, rank = adapter_up_factors.shape[:2]
    count = adapter_storage_slot.shape[0]
    half = chips * tok_dev
    total = 2 * half
    room = 4 if total <= 16 else 40
    same_core = [[c + 2 * i for i in range(chips)] for c in range(2)]
    pairs = [(i, i ^ 1) for i in range(devices)]
    parts = PARTS if hidden_dev % (256 * PARTS) == 0 else 1
    units = hidden_dev // parts

    wg, wu, wd = far(gate_weight), far(up_weight), far(down_weight)
    d = far(adapter_down_factors.reshape(count * rank, hidden_dev))
    u = far(adapter_up_factors.reshape(kept * rank, width))
    weight_mib = -(-2 * width * hidden_dev >> 20)

    (sent,) = call(
        pack_kernel,
        (token_adapter_index, far(adapter_storage_slot), far(tokens), far(cotangent)),
        (((chips, 2, width + SPLIT), bf16),),
        room,
        specs=[SMEM] + [HBM] * 3,
        scratch=[
            pltpu.SMEM(adapter_storage_slot.shape, jnp.int32),
            pltpu.VMEM(tokens.shape, bf16),
            pltpu.VMEM(cotangent.shape, bf16),
            pltpu.SemaphoreType.DMA((3,)),
        ],
    )
    own = lax.all_to_all(sent, "tensor", 0, 0, axis_index_groups=same_core, tiled=True)
    sib = lax.ppermute(own, "tensor", pairs)
    gathered = jnp.concatenate((own, sib), axis=0).reshape(total, 2, width + SPLIT)
    x = gathered[:, 0, :width]
    c = gathered[:, 1, :width]
    code = gathered[:, 0, width : width + 2].astype(f32)
    slots = code[:, 0:1] * SPLIT + code[:, 1:2]

    sems = pltpu.SemaphoreType.DMA
    gate, up, hid, pay, base, pull, wg, d, u = call(
        functools.partial(forward_kernel, rank, parts),
        (x, c, slots, wg, wu, wd, d, u),
        (
            ((total, hidden_dev), f32),
            ((total, hidden_dev), f32),
            ((total, hidden_dev), bf16),
            ((devices, half, -(-4 * rank // 128) * 128), f32),
            ((total, width), f32),
            ((total, hidden_dev), f32),
            pltpu.VMEM(wg.shape, bf16),
            pltpu.VMEM(d.shape, bf16),
            pltpu.VMEM(u.shape, bf16),
        ),
        room + 6 + -(-2 * weight_mib // parts),
        specs=[VMEM] * 3 + [HBM] * 5,
        scratch=[
            pltpu.VMEM((width, units), bf16),
            pltpu.VMEM((units, width), bf16),
            sems((parts, width // fit(width, PIECE // units))),
            sems((parts, width // fit(width, PIECE // units))),
            sems((parts, units // fit(units, PIECE // width))),
            sems((2,)),
        ],
    )
    got = lax.all_to_all(pay, "tensor", 0, 0)
    mine, theirs, left, weighted = call(
        functools.partial(backward_kernel, rank),
        (got, slots, gate, up, base, pull, held(wg), wu, held(d), held(u)),
        (
            ((2, half, width), f32),
            ((2, half, width), bf16),
            ((total, count * rank), bf16),
            ((2 * total, kept * rank), bf16),
        ),
        room + 6 + weight_mib,
        specs=[VMEM] * 7 + [HBM, VMEM, VMEM],
        scratch=[pltpu.VMEM(wu.shape, bf16), sems((width // fit(width, 1024),))],
    )
    summed = mine + lax.ppermute(theirs, "tensor", pairs).astype(f32)
    summed = jnp.transpose(
        summed.astype(bf16).reshape(2, chips, tok_dev, width), (1, 0, 2, 3)
    ).reshape(chips, 2 * tok_dev, width)
    back = lax.all_to_all(summed, "tensor", 0, 0, axis_index_groups=same_core, tiled=True)
    down_grad, up_factor_gradient = call(
        factor_kernel,
        (left, hid, weighted, c),
        (((count * rank, hidden_dev), bf16), ((kept * rank, width), bf16)),
        room,
        flops=2 * total * count * rank * hidden_dev,
        nbytes=2 * (count * rank * hidden_dev + kept * rank * width),
    )
    final = jnp.sum(back.astype(f32).reshape(chips, 2, tok_dev, width), axis=0).astype(bf16)
    return (
        final[0],
        final[1],
        down_grad.reshape(count, rank, hidden_dev),
        up_factor_gradient.reshape(kept, rank, width),
    )


def solution(mesh):
    in_specs = (
        P(("parts", "tensor"), None),
        P(("parts", "tensor"), None),
        P(("parts", "tensor")),
        P(),
        P(None, "tensor"),
        P(None, "tensor"),
        P("tensor", None),
        P(None, None, "tensor"),
        P("tensor", None, None),
    )
    out_specs = (
        P(("parts", "tensor"), None),
        P(("parts", "tensor"), None),
        P("parts", None, "tensor"),
        P(("parts", "tensor"), None, None),
    )
    return jax.shard_map(
        per_device, mesh=mesh, in_specs=in_specs, out_specs=out_specs, check_vma=False
    )
```

```python
import functools

import jax
import jax.numpy as jnp
from jax import lax
from jax.experimental import pallas as pl
from jax.experimental.pallas import tpu as pltpu
from jax.sharding import PartitionSpec as P

adapter_scale = 2.0
f32 = jnp.float32
bf16 = jnp.bfloat16
AHEAD = 8
PARTS = 2
PIECE = 1 << 20
SPLIT = 128
VMEM = pl.BlockSpec(memory_space=pltpu.VMEM)
SMEM = pl.BlockSpec(memory_space=pltpu.SMEM)
HBM = pl.BlockSpec(memory_space=pltpu.HBM)
NT = (((1,), (1,)), ((), ()))
TN = (((0,), (0,)), ((), ()))


def params(mib):
    return pltpu.CompilerParams(vmem_limit_bytes=mib << 20)


def fit(size, want):
    return want if size % want == 0 else size


def slot_mask(slot, first, columns, rank):
    col = lax.broadcasted_iota(jnp.int32, (slot.shape[0], columns), 1) // rank
    return slot.astype(jnp.int32) == col + first


def fold_matrix(columns, rank, by_row):
    shape = (columns, rank) if by_row else (rank, columns)
    c = lax.broadcasted_iota(jnp.int32, shape, 0 if by_row else 1)
    r = lax.broadcasted_iota(jnp.int32, shape, 1 if by_row else 0)
    return jnp.where(c % rank == r, 1.0, 0.0).astype(bf16)


def halves(v):
    high = v.astype(bf16)
    return high, (v - high.astype(f32)).astype(bf16)


def dot(a, b, dims=(((1,), (0,)), ((), ()))):
    return lax.dot_general(a, b, dims, preferred_element_type=f32)


def dot2(v, b, dims=(((1,), (0,)), ((), ()))):
    high, low = halves(v)
    return dot(high, b, dims) + dot(low, b, dims)


class Stream:
    def __init__(self, ahead):
        self.moves, self.ahead, self.taken, self.begun = [], ahead, 0, 0

    def add(self, src, dst, sem):
        self.moves.append(pltpu.make_async_copy(src, dst, sem))

    def fill(self):
        while self.begun < min(self.taken + self.ahead, len(self.moves)):
            self.moves[self.begun].start()
            self.begun += 1

    def take(self, count=1):
        for _ in range(count):
            self.fill()
            self.moves[self.taken].wait()
            self.taken += 1
        self.fill()


def pack_kernel(
    index_ref, table_hbm, tokens_hbm, cotangent_hbm, out_ref,
    table_ref, tokens_ref, cotangent_ref, sems,
):
    moves = [
        pltpu.make_async_copy(a, b, sems.at[i])
        for i, (a, b) in enumerate(
            (
                (table_hbm, table_ref),
                (tokens_hbm, tokens_ref),
                (cotangent_hbm, cotangent_ref),
            )
        )
    ]
    for m in moves:
        m.start()
    for m in moves:
        m.wait()
    width = tokens_ref.shape[1]
    slot = table_ref[index_ref[0]]
    lane = lax.broadcasted_iota(jnp.int32, (1, SPLIT), 1)
    digits = jnp.where(lane == 0, slot // SPLIT, jnp.where(lane == 1, slot % SPLIT, 0))
    digits = digits.astype(f32).astype(bf16)
    for i in range(out_ref.shape[0]):
        out_ref[i, 0:1, :width] = tokens_ref[...]
        out_ref[i, 1:2, :width] = cotangent_ref[...]
        out_ref[i, 0:1, width:] = digits
        out_ref[i, 1:2, width:] = digits


def blocks(size, step):
    return [pl.ds(i * step, step) for i in range(size // step)]


def forward_kernel(
    rank, parts,
    x_ref, c_ref, slot_ref, wg_hbm, wu_hbm, wd_hbm, d_hbm, u_hbm,
    gate_ref, up_ref, hid_ref, pay_ref, base_ref, pull_ref, wg_ref, d_ref, u_ref,
    wu_ref, wd_ref, sg, su, sd, sf,
):
    total, width = x_ref.shape
    hidden_dev = wg_ref.shape[1]
    units = hidden_dev // parts
    tall = fit(width, PIECE // units)
    flat = fit(units, PIECE // width)
    stream = Stream(AHEAD)
    stream.add(u_hbm, u_ref, sf.at[0])
    for p, f in enumerate(blocks(hidden_dev, units)):
        for j, k in enumerate(blocks(width, tall)):
            stream.add(wg_hbm.at[k, f], wg_ref.at[k, f], sg.at[p, j])
        for j, k in enumerate(blocks(width, tall)):
            stream.add(wu_hbm.at[k, f], wu_ref.at[k], su.at[p, j])
        if p == parts - 1:
            stream.add(d_hbm, d_ref, sf.at[1])
        for j, k in enumerate(blocks(units, flat)):
            at = pl.ds(p * units + j * flat, flat)
            stream.add(wd_hbm.at[at], wd_ref.at[k], sd.at[p, j])
    stream.fill()
    half = total // 2
    slot = slot_ref[...]

    stream.take()
    kept = u_ref.shape[0]
    first = lax.axis_index("tensor") * (kept // rank)
    pulled = dot(c_ref[...], u_ref[...], NT)
    pulled = jnp.where(slot_mask(slot, first, kept, rank), pulled, 0.0)
    rank_out = adapter_scale * dot2(pulled, fold_matrix(kept, rank, True))

    def project(w_ref, f):
        acc = jnp.zeros((total, units), f32)
        for k in blocks(width, fit(width, 2 * tall)):
            stream.take(k.size // tall)
            acc = acc + dot(x_ref[:, k], w_ref[k, f])
        return acc

    step = fit(width, 2048)
    for p, f in enumerate(blocks(hidden_dev, units)):
        gate = project(wg_ref, f)
        gate_ref[:, f] = gate
        up = project(wu_ref, slice(None))
        up_ref[:, f] = up
        hid = (gate * jax.nn.sigmoid(gate) * up).astype(bf16)
        hid_ref[:, f] = hid
        if p == parts - 1:
            stream.take()
            columns = d_ref.shape[0]
            met = dot(hid_ref[...], d_ref[...], NT)
            met = jnp.where(slot_mask(slot, 0, columns, rank), met, 0.0)
            rank_in = dot2(met, fold_matrix(columns, rank, True))
        stream.take(units // flat)
        pull_ref[:, f] = dot(c_ref[...], wd_ref[...], NT)
        for s in blocks(width, step):
            part = dot(hid, wd_ref[:, s])
            base_ref[:, s] = part if p == 0 else base_ref[:, s] + part

    both = jnp.concatenate((rank_in, rank_out), axis=1)
    swap = lax.axis_index("tensor") % 2
    own, sib = both[:half], both[half:]
    pay = jnp.concatenate(
        (
            jnp.where(swap == 0, own, sib),
            jnp.where(swap == 0, sib, own),
            jnp.zeros((half, pay_ref.shape[2] - 4 * rank), f32),
        ),
        axis=1,
    )
    for i in range(pay_ref.shape[0]):
        pay_ref[i] = pay


def backward_kernel(
    rank,
    got_ref, slot_ref, gate_ref, up_ref, base_ref, pull_ref, wg_ref, wu_hbm, d_ref, u_ref,
    own_ref, sib_ref, left_ref, weighted_ref,
    wu_ref, su,
):
    total, hidden_dev = gate_ref.shape
    width = wg_ref.shape[0]
    piece = fit(width, 1024)
    stream = Stream(AHEAD)
    for j, k in enumerate(blocks(width, piece)):
        stream.add(wu_hbm.at[k], wu_ref.at[k], su.at[j])
    stream.fill()
    half = total // 2
    columns = d_ref.shape[0]
    kept = u_ref.shape[0]
    got = jnp.sum(got_ref[...], axis=0)
    swap = lax.axis_index("tensor") % 2
    a, b = got[:, : 2 * rank], got[:, 2 * rank : 4 * rank]
    both = jnp.concatenate(
        (jnp.where(swap == 0, a, b), jnp.where(swap == 0, b, a)), axis=0
    )
    rank_in = both[:, :rank]
    rank_out = both[:, rank:].astype(bf16)
    spread = dot(rank_out, fold_matrix(columns, rank, False))
    slot = slot_ref[...]
    left = jnp.where(slot_mask(slot, 0, columns, rank), spread, 0.0).astype(bf16)
    left_ref[...] = left
    grad = pull_ref[...] + dot(left, d_ref[...])
    gate = gate_ref[...]
    up = up_ref[...]
    sig = jax.nn.sigmoid(gate)
    gg = (grad * up * sig * (1.0 + gate * (1.0 - sig))).astype(bf16)
    gu = (grad * (gate * sig)).astype(bf16)
    first = lax.axis_index("tensor") * (kept // rank)
    mine = slot_mask(slot, first, kept, rank)
    high, low = halves(rank_in)
    fold = fold_matrix(kept, rank, False)
    high = jnp.where(mine, dot(high, fold), 0.0).astype(bf16)
    low = jnp.where(mine, dot(low, fold), 0.0).astype(bf16)
    weighted_ref[...] = jnp.concatenate((high, low), axis=0)
    for s in blocks(width, 2 * piece):
        us = u_ref[:, s]
        adapted = adapter_scale * (dot(high, us) + dot(low, us))
        out = base_ref[:, s] + adapted.astype(bf16).astype(f32)
        own_ref[0, :, s] = out[:half]
        sib_ref[0, :, s] = out[half:].astype(bf16)
        stream.take(2)
        for i in range(8):
            t = pl.ds(s.start + i * piece // 4, piece // 4)
            inp = dot(gg, wg_ref[t, :], NT) + dot(gu, wu_ref[t, :], NT)
            own_ref[1, :, t] = inp[:half]
            sib_ref[1, :, t] = inp[half:].astype(bf16)


def factor_kernel(left_ref, hid_ref, weighted_ref, c_ref, down_ref, upg_ref):
    columns = down_ref.shape[0]
    rows = fit(columns, 256)
    for i in range(columns // rows):
        s = pl.ds(i * rows, rows)
        down_ref[s, :] = dot(left_ref[:, s], hid_ref[...], TN).astype(bf16)
    width = c_ref.shape[1]
    chunk = fit(width, 1024)
    total = c_ref.shape[0]
    for i in range(width // chunk):
        s = pl.ds(i * chunk, chunk)
        cs = c_ref[:, s]
        both = dot(weighted_ref[:total], cs, TN) + dot(weighted_ref[total:], cs, TN)
        upg_ref[:, s] = (adapter_scale * both).astype(bf16)


def combine_kernel(own_ref, got_ref, out_ref):
    for i in range(own_ref.shape[0]):
        both = own_ref[i] + got_ref[i].astype(f32)
        out_ref[:, i, :] = both.astype(bf16)


def finish_kernel(back_ref, mixed_ref, grad_ref):
    total = jnp.sum(back_ref[...].astype(f32), axis=0).astype(bf16)
    rows = mixed_ref.shape[0]
    mixed_ref[...] = total[:rows]
    grad_ref[...] = total[rows:]


def call(kernel, args, outs, mib, specs=None, out_specs=None, flops=0, nbytes=0, scratch=()):
    return pl.pallas_call(
        kernel,
        in_specs=specs or [VMEM] * len(args),
        out_specs=out_specs or [VMEM] * len(outs),
        out_shape=[jax.ShapeDtypeStruct(*o) if isinstance(o, tuple) else o for o in outs],
        scratch_shapes=scratch,
        compiler_params=params(mib),
        cost_estimate=pl.CostEstimate(flops=flops, bytes_accessed=nbytes, transcendentals=0),
    )(*args)


def held(x):
    return pltpu.with_memory_space_constraint(x, pltpu.VMEM)


def far(x):
    return pltpu.with_memory_space_constraint(x, pltpu.HBM)


def per_device(
    tokens,
    cotangent,
    token_adapter_index,
    adapter_storage_slot,
    gate_weight,
    up_weight,
    down_weight,
    adapter_down_factors,
    adapter_up_factors,
):
    devices = lax.axis_size("tensor")
    chips = devices // 2
    tok_dev, width = tokens.shape
    hidden_dev = gate_weight.shape[1]
    kept, rank = adapter_up_factors.shape[:2]
    count = adapter_storage_slot.shape[0]
    half = chips * tok_dev
    total = 2 * half
    room = 4 if total <= 16 else 40
    same_core = [[c + 2 * i for i in range(chips)] for c in range(2)]
    pairs = [(i, i ^ 1) for i in range(devices)]
    parts = PARTS if hidden_dev % (256 * PARTS) == 0 else 1
    units = hidden_dev // parts

    wg, wu, wd = far(gate_weight), far(up_weight), far(down_weight)
    d = far(adapter_down_factors.reshape(count * rank, hidden_dev))
    u = far(adapter_up_factors.reshape(kept * rank, width))
    weight_mib = -(-2 * width * hidden_dev >> 20)

    (sent,) = call(
        pack_kernel,
        (token_adapter_index, far(adapter_storage_slot), far(tokens), far(cotangent)),
        (((chips, 2, width + SPLIT), bf16),),
        room,
        specs=[SMEM] + [HBM] * 3,
        scratch=[
            pltpu.SMEM(adapter_storage_slot.shape, jnp.int32),
            pltpu.VMEM(tokens.shape, bf16),
            pltpu.VMEM(cotangent.shape, bf16),
            pltpu.SemaphoreType.DMA((3,)),
        ],
    )
    own = lax.all_to_all(sent, "tensor", 0, 0, axis_index_groups=same_core, tiled=True)
    sib = lax.ppermute(own, "tensor", pairs)
    gathered = jnp.concatenate((own, sib), axis=0).reshape(total, 2, width + SPLIT)
    x = gathered[:, 0, :width]
    c = gathered[:, 1, :width]
    code = gathered[:, 0, width : width + 2].astype(f32)
    slots = code[:, 0:1] * SPLIT + code[:, 1:2]

    sems = pltpu.SemaphoreType.DMA
    gate, up, hid, pay, base, pull, wg, d, u = call(
        functools.partial(forward_kernel, rank, parts),
        (x, c, slots, wg, wu, wd, d, u),
        (
            ((total, hidden_dev), f32),
            ((total, hidden_dev), f32),
            ((total, hidden_dev), bf16),
            ((devices, half, -(-4 * rank // 128) * 128), f32),
            ((total, width), f32),
            ((total, hidden_dev), f32),
            pltpu.VMEM(wg.shape, bf16),
            pltpu.VMEM(d.shape, bf16),
            pltpu.VMEM(u.shape, bf16),
        ),
        room + 6 + -(-2 * weight_mib // parts),
        specs=[VMEM] * 3 + [HBM] * 5,
        scratch=[
            pltpu.VMEM((width, units), bf16),
            pltpu.VMEM((units, width), bf16),
            sems((parts, width // fit(width, PIECE // units))),
            sems((parts, width // fit(width, PIECE // units))),
            sems((parts, units // fit(units, PIECE // width))),
            sems((2,)),
        ],
    )
    got = lax.all_to_all(pay, "tensor", 0, 0)
    mine, theirs, left, weighted = call(
        functools.partial(backward_kernel, rank),
        (got, slots, gate, up, base, pull, held(wg), wu, held(d), held(u)),
        (
            ((2, half, width), f32),
            ((2, half, width), bf16),
            ((total, count * rank), bf16),
            ((2 * total, kept * rank), bf16),
        ),
        room + 6 + weight_mib,
        specs=[VMEM] * 7 + [HBM, VMEM, VMEM],
        scratch=[pltpu.VMEM(wu.shape, bf16), sems((width // fit(width, 1024),))],
    )
    (summed,) = call(
        combine_kernel,
        (mine, lax.ppermute(theirs, "tensor", pairs)),
        (((half, 2, width), bf16),),
        room,
    )
    back = lax.all_to_all(summed, "tensor", 0, 0, axis_index_groups=same_core, tiled=True)
    down_grad, up_factor_gradient = call(
        factor_kernel,
        (left, hid, weighted, c),
        (((count * rank, hidden_dev), bf16), ((kept * rank, width), bf16)),
        room,
        flops=2 * total * count * rank * hidden_dev,
        nbytes=2 * (count * rank * hidden_dev + kept * rank * width),
    )
    mixed, input_grad = call(
        finish_kernel,
        (back,),
        (((tok_dev, width), bf16), ((tok_dev, width), bf16)),
        room,
    )
    return (
        mixed,
        input_grad,
        down_grad.reshape(count, rank, hidden_dev),
        up_factor_gradient.reshape(kept, rank, width),
    )


def solution(mesh):
    in_specs = (
        P(("parts", "tensor"), None),
        P(("parts", "tensor"), None),
        P(("parts", "tensor")),
        P(),
        P(None, "tensor"),
        P(None, "tensor"),
        P("tensor", None),
        P(None, None, "tensor"),
        P("tensor", None, None),
    )
    out_specs = (
        P(("parts", "tensor"), None),
        P(("parts", "tensor"), None),
        P("parts", None, "tensor"),
        P(("parts", "tensor"), None, None),
    )
    return jax.shard_map(
        per_device, mesh=mesh, in_specs=in_specs, out_specs=out_specs, check_vma=False
    )
```

```python
import functools

import jax
import jax.numpy as jnp
from jax import lax
from jax.experimental import pallas as pl
from jax.experimental.pallas import tpu as pltpu
from jax.sharding import PartitionSpec as P

adapter_scale = 2.0
f32 = jnp.float32
bf16 = jnp.bfloat16
AHEAD = 8
PARTS = 2
PIECE = 1 << 20
SPLIT = 128
VMEM = pl.BlockSpec(memory_space=pltpu.VMEM)
SMEM = pl.BlockSpec(memory_space=pltpu.SMEM)
HBM = pl.BlockSpec(memory_space=pltpu.HBM)
NT = (((1,), (1,)), ((), ()))
TN = (((0,), (0,)), ((), ()))


def params(mib):
    return pltpu.CompilerParams(vmem_limit_bytes=mib << 20)


def fit(size, want):
    return want if size % want == 0 else size


def slot_mask(slot, first, columns, rank):
    col = lax.broadcasted_iota(jnp.int32, (slot.shape[0], columns), 1) // rank
    return slot.astype(jnp.int32) == col + first


def fold_matrix(columns, rank, by_row):
    shape = (columns, rank) if by_row else (rank, columns)
    c = lax.broadcasted_iota(jnp.int32, shape, 0 if by_row else 1)
    r = lax.broadcasted_iota(jnp.int32, shape, 1 if by_row else 0)
    return jnp.where(c % rank == r, 1.0, 0.0).astype(bf16)


def halves(v):
    high = v.astype(bf16)
    return high, (v - high.astype(f32)).astype(bf16)


def dot(a, b, dims=(((1,), (0,)), ((), ()))):
    return lax.dot_general(a, b, dims, preferred_element_type=f32)


def dot2(v, b, dims=(((1,), (0,)), ((), ()))):
    high, low = halves(v)
    return dot(high, b, dims) + dot(low, b, dims)


class Stream:
    def __init__(self, ahead):
        self.moves, self.ahead, self.taken, self.begun = [], ahead, 0, 0

    def add(self, src, dst, sem):
        self.moves.append(pltpu.make_async_copy(src, dst, sem))

    def fill(self):
        while self.begun < min(self.taken + self.ahead, len(self.moves)):
            self.moves[self.begun].start()
            self.begun += 1

    def take(self, count=1):
        for _ in range(count):
            self.fill()
            self.moves[self.taken].wait()
            self.taken += 1
        self.fill()


def pack_kernel(
    index_ref, table_hbm, tokens_hbm, cotangent_hbm, out_ref,
    table_ref, tokens_ref, cotangent_ref, sems,
):
    moves = [
        pltpu.make_async_copy(a, b, sems.at[i])
        for i, (a, b) in enumerate(
            (
                (table_hbm, table_ref),
                (tokens_hbm, tokens_ref),
                (cotangent_hbm, cotangent_ref),
            )
        )
    ]
    for m in moves:
        m.start()
    for m in moves:
        m.wait()
    slot = table_ref[index_ref[0]]
    lane = lax.broadcasted_iota(jnp.int32, (2, SPLIT), 1)
    digits = jnp.where(lane == 0, slot // SPLIT, jnp.where(lane == 1, slot % SPLIT, 0))
    rows = jnp.concatenate(
        (tokens_ref[...].astype(f32), cotangent_ref[...].astype(f32)), axis=0
    )
    rows = jnp.concatenate((rows, digits.astype(f32)), axis=1).astype(bf16)
    for i in range(out_ref.shape[0]):
        out_ref[i] = rows


def blocks(size, step):
    return [pl.ds(i * step, step) for i in range(size // step)]


def forward_kernel(
    rank, parts,
    x_ref, c_ref, slot_ref, wg_hbm, wu_hbm, wd_hbm, d_hbm, u_hbm,
    gate_ref, up_ref, hid_ref, pay_ref, base_ref, pull_ref, wg_ref, d_ref, u_ref,
    wu_ref, wd_ref, sg, su, sd, sf,
):
    total, width = x_ref.shape
    hidden_dev = wg_ref.shape[1]
    units = hidden_dev // parts
    tall = fit(width, PIECE // units)
    flat = fit(units, PIECE // width)
    stream = Stream(AHEAD)
    stream.add(u_hbm, u_ref, sf.at[0])
    for p, f in enumerate(blocks(hidden_dev, units)):
        for j, k in enumerate(blocks(width, tall)):
            stream.add(wg_hbm.at[k, f], wg_ref.at[k, f], sg.at[p, j])
        for j, k in enumerate(blocks(width, tall)):
            stream.add(wu_hbm.at[k, f], wu_ref.at[k], su.at[p, j])
        if p == parts - 1:
            stream.add(d_hbm, d_ref, sf.at[1])
        for j, k in enumerate(blocks(units, flat)):
            at = pl.ds(p * units + j * flat, flat)
            stream.add(wd_hbm.at[at], wd_ref.at[k], sd.at[p, j])
    stream.fill()
    half = total // 2
    slot = slot_ref[...]

    stream.take()
    kept = u_ref.shape[0]
    first = lax.axis_index("tensor") * (kept // rank)
    pulled = dot(c_ref[...], u_ref[...], NT)
    pulled = jnp.where(slot_mask(slot, first, kept, rank), pulled, 0.0)
    rank_out = adapter_scale * dot2(pulled, fold_matrix(kept, rank, True))

    def project(w_ref, f):
        acc = jnp.zeros((total, units), f32)
        for k in blocks(width, fit(width, 2 * tall)):
            stream.take(k.size // tall)
            acc = acc + dot(x_ref[:, k], w_ref[k, f])
        return acc

    step = fit(width, 2048)
    for p, f in enumerate(blocks(hidden_dev, units)):
        gate = project(wg_ref, f)
        gate_ref[:, f] = gate
        up = project(wu_ref, slice(None))
        up_ref[:, f] = up
        hid = (gate * jax.nn.sigmoid(gate) * up).astype(bf16)
        hid_ref[:, f] = hid
        if p == parts - 1:
            stream.take()
            columns = d_ref.shape[0]
            met = dot(hid_ref[...], d_ref[...], NT)
            met = jnp.where(slot_mask(slot, 0, columns, rank), met, 0.0)
            rank_in = dot2(met, fold_matrix(columns, rank, True))
        stream.take(units // flat)
        pull_ref[:, f] = dot(c_ref[...], wd_ref[...], NT)
        for s in blocks(width, step):
            part = dot(hid, wd_ref[:, s])
            base_ref[:, s] = part if p == 0 else base_ref[:, s] + part

    both = jnp.concatenate((rank_in, rank_out), axis=1)
    swap = lax.axis_index("tensor") % 2
    own, sib = both[:half], both[half:]
    pay = jnp.concatenate(
        (
            jnp.where(swap == 0, own, sib),
            jnp.where(swap == 0, sib, own),
            jnp.zeros((half, pay_ref.shape[2] - 4 * rank), f32),
        ),
        axis=1,
    )
    for i in range(pay_ref.shape[0]):
        pay_ref[i] = pay


def backward_kernel(
    rank,
    got_ref, slot_ref, gate_ref, up_ref, base_ref, pull_ref, wg_ref, wu_hbm, d_ref, u_ref,
    own_ref, sib_ref, left_ref, weighted_ref,
    wu_ref, su,
):
    total, hidden_dev = gate_ref.shape
    width = wg_ref.shape[0]
    piece = fit(width, 1024)
    stream = Stream(AHEAD)
    for j, k in enumerate(blocks(width, piece)):
        stream.add(wu_hbm.at[k], wu_ref.at[k], su.at[j])
    stream.fill()
    half = total // 2
    columns = d_ref.shape[0]
    kept = u_ref.shape[0]
    got = jnp.sum(got_ref[...], axis=0)
    swap = lax.axis_index("tensor") % 2
    a, b = got[:, : 2 * rank], got[:, 2 * rank : 4 * rank]
    both = jnp.concatenate(
        (jnp.where(swap == 0, a, b), jnp.where(swap == 0, b, a)), axis=0
    )
    rank_in = both[:, :rank]
    rank_out = both[:, rank:].astype(bf16)
    spread = dot(rank_out, fold_matrix(columns, rank, False))
    slot = slot_ref[...]
    left = jnp.where(slot_mask(slot, 0, columns, rank), spread, 0.0).astype(bf16)
    left_ref[...] = left
    grad = pull_ref[...] + dot(left, d_ref[...])
    gate = gate_ref[...]
    up = up_ref[...]
    sig = jax.nn.sigmoid(gate)
    gg = (grad * up * sig * (1.0 + gate * (1.0 - sig))).astype(bf16)
    gu = (grad * (gate * sig)).astype(bf16)
    first = lax.axis_index("tensor") * (kept // rank)
    mine = slot_mask(slot, first, kept, rank)
    high, low = halves(rank_in)
    fold = fold_matrix(kept, rank, False)
    high = jnp.where(mine, dot(high, fold), 0.0).astype(bf16)
    low = jnp.where(mine, dot(low, fold), 0.0).astype(bf16)
    weighted_ref[...] = jnp.concatenate((high, low), axis=0)
    for s in blocks(width, 2 * piece):
        us = u_ref[:, s]
        adapted = adapter_scale * (dot(high, us) + dot(low, us))
        out = base_ref[:, s] + adapted.astype(bf16).astype(f32)
        own_ref[0, :, s] = out[:half]
        sib_ref[0, :, s] = out[half:].astype(bf16)
        stream.take(2)
        for i in range(8):
            t = pl.ds(s.start + i * piece // 4, piece // 4)
            inp = dot(gg, wg_ref[t, :], NT) + dot(gu, wu_ref[t, :], NT)
            own_ref[1, :, t] = inp[:half]
            sib_ref[1, :, t] = inp[half:].astype(bf16)


def factor_kernel(left_ref, hid_ref, weighted_ref, c_ref, down_ref, upg_ref):
    columns = down_ref.shape[0]
    rows = fit(columns, 256)
    for i in range(columns // rows):
        s = pl.ds(i * rows, rows)
        down_ref[s, :] = dot(left_ref[:, s], hid_ref[...], TN).astype(bf16)
    width = c_ref.shape[1]
    chunk = fit(width, 1024)
    total = c_ref.shape[0]
    for i in range(width // chunk):
        s = pl.ds(i * chunk, chunk)
        cs = c_ref[:, s]
        both = dot(weighted_ref[:total], cs, TN) + dot(weighted_ref[total:], cs, TN)
        upg_ref[:, s] = (adapter_scale * both).astype(bf16)


def call(kernel, args, outs, mib, specs=None, out_specs=None, flops=0, nbytes=0, scratch=()):
    return pl.pallas_call(
        kernel,
        in_specs=specs or [VMEM] * len(args),
        out_specs=out_specs or [VMEM] * len(outs),
        out_shape=[jax.ShapeDtypeStruct(*o) if isinstance(o, tuple) else o for o in outs],
        scratch_shapes=scratch,
        compiler_params=params(mib),
        cost_estimate=pl.CostEstimate(flops=flops, bytes_accessed=nbytes, transcendentals=0),
    )(*args)


def held(x):
    return pltpu.with_memory_space_constraint(x, pltpu.VMEM)


def far(x):
    return pltpu.with_memory_space_constraint(x, pltpu.HBM)


def per_device(
    tokens,
    cotangent,
    token_adapter_index,
    adapter_storage_slot,
    gate_weight,
    up_weight,
    down_weight,
    adapter_down_factors,
    adapter_up_factors,
):
    devices = lax.axis_size("tensor")
    chips = devices // 2
    tok_dev, width = tokens.shape
    hidden_dev = gate_weight.shape[1]
    kept, rank = adapter_up_factors.shape[:2]
    count = adapter_storage_slot.shape[0]
    half = chips * tok_dev
    total = 2 * half
    room = 4 if total <= 16 else 40
    same_core = [[c + 2 * i for i in range(chips)] for c in range(2)]
    pairs = [(i, i ^ 1) for i in range(devices)]
    parts = PARTS if hidden_dev % (256 * PARTS) == 0 else 1
    units = hidden_dev // parts

    wg, wu, wd = far(gate_weight), far(up_weight), far(down_weight)
    d = far(adapter_down_factors.reshape(count * rank, hidden_dev))
    u = far(adapter_up_factors.reshape(kept * rank, width))
    weight_mib = -(-2 * width * hidden_dev >> 20)

    (sent,) = call(
        pack_kernel,
        (token_adapter_index, far(adapter_storage_slot), far(tokens), far(cotangent)),
        (((chips, 2, width + SPLIT), bf16),),
        room,
        specs=[SMEM] + [HBM] * 3,
        scratch=[
            pltpu.SMEM(adapter_storage_slot.shape, jnp.int32),
            pltpu.VMEM(tokens.shape, bf16),
            pltpu.VMEM(cotangent.shape, bf16),
            pltpu.SemaphoreType.DMA((3,)),
        ],
    )
    own = lax.all_to_all(sent, "tensor", 0, 0, axis_index_groups=same_core, tiled=True)
    sib = lax.ppermute(own, "tensor", pairs)
    gathered = jnp.concatenate((own, sib), axis=0).reshape(total, 2, width + SPLIT)
    x = gathered[:, 0, :width]
    c = gathered[:, 1, :width]
    code = gathered[:, 0, width : width + 2].astype(f32)
    slots = code[:, 0:1] * SPLIT + code[:, 1:2]

    sems = pltpu.SemaphoreType.DMA
    gate, up, hid, pay, base, pull, wg, d, u = call(
        functools.partial(forward_kernel, rank, parts),
        (x, c, slots, wg, wu, wd, d, u),
        (
            ((total, hidden_dev), f32),
            ((total, hidden_dev), f32),
            ((total, hidden_dev), bf16),
            ((devices, half, -(-4 * rank // 128) * 128), f32),
            ((total, width), f32),
            ((total, hidden_dev), f32),
            pltpu.VMEM(wg.shape, bf16),
            pltpu.VMEM(d.shape, bf16),
            pltpu.VMEM(u.shape, bf16),
        ),
        room + 6 + -(-2 * weight_mib // parts),
        specs=[VMEM] * 3 + [HBM] * 5,
        scratch=[
            pltpu.VMEM((width, units), bf16),
            pltpu.VMEM((units, width), bf16),
            sems((parts, width // fit(width, PIECE // units))),
            sems((parts, width // fit(width, PIECE // units))),
            sems((parts, units // fit(units, PIECE // width))),
            sems((2,)),
        ],
    )
    got = lax.all_to_all(pay, "tensor", 0, 0)
    mine, theirs, left, weighted = call(
        functools.partial(backward_kernel, rank),
        (got, slots, gate, up, base, pull, held(wg), wu, held(d), held(u)),
        (
            ((2, half, width), f32),
            ((2, half, width), bf16),
            ((total, count * rank), bf16),
            ((2 * total, kept * rank), bf16),
        ),
        room + 6 + weight_mib,
        specs=[VMEM] * 7 + [HBM, VMEM, VMEM],
        scratch=[pltpu.VMEM(wu.shape, bf16), sems((width // fit(width, 1024),))],
    )
    summed = mine + lax.ppermute(theirs, "tensor", pairs).astype(f32)
    summed = jnp.transpose(
        summed.astype(bf16).reshape(2, chips, tok_dev, width), (1, 0, 2, 3)
    ).reshape(chips, 2 * tok_dev, width)
    back = lax.all_to_all(summed, "tensor", 0, 0, axis_index_groups=same_core, tiled=True)
    down_grad, up_factor_gradient = call(
        factor_kernel,
        (left, hid, weighted, c),
        (((count * rank, hidden_dev), bf16), ((kept * rank, width), bf16)),
        room,
        flops=2 * total * count * rank * hidden_dev,
        nbytes=2 * (count * rank * hidden_dev + kept * rank * width),
    )
    final = jnp.sum(back.astype(f32).reshape(chips, 2, tok_dev, width), axis=0).astype(bf16)
    return (
        final[0],
        final[1],
        down_grad.reshape(count, rank, hidden_dev),
        up_factor_gradient.reshape(kept, rank, width),
    )


def solution(mesh):
    in_specs = (
        P(("parts", "tensor"), None),
        P(("parts", "tensor"), None),
        P(("parts", "tensor")),
        P(),
        P(None, "tensor"),
        P(None, "tensor"),
        P("tensor", None),
        P(None, None, "tensor"),
        P("tensor", None, None),
    )
    out_specs = (
        P(("parts", "tensor"), None),
        P(("parts", "tensor"), None),
        P("parts", None, "tensor"),
        P(("parts", "tensor"), None, None),
    )
    return jax.shard_map(
        per_device, mesh=mesh, in_specs=in_specs, out_specs=out_specs, check_vma=False
    )
```

```python
import functools

import jax
import jax.numpy as jnp
from jax import lax
from jax.experimental import pallas as pl
from jax.experimental.pallas import tpu as pltpu
from jax.sharding import PartitionSpec as P

adapter_scale = 2.0
f32 = jnp.float32
bf16 = jnp.bfloat16
AHEAD = 8
PARTS = 2
PIECE = 1 << 20
SPLIT = 128
VMEM = pl.BlockSpec(memory_space=pltpu.VMEM)
SMEM = pl.BlockSpec(memory_space=pltpu.SMEM)
HBM = pl.BlockSpec(memory_space=pltpu.HBM)
NT = (((1,), (1,)), ((), ()))
TN = (((0,), (0,)), ((), ()))


def params(mib):
    return pltpu.CompilerParams(vmem_limit_bytes=mib << 20)


def fit(size, want):
    return want if size % want == 0 else size


def slot_mask(slot, first, columns, rank):
    col = lax.broadcasted_iota(jnp.int32, (slot.shape[0], columns), 1) // rank
    return slot.astype(jnp.int32) == col + first


def fold_matrix(columns, rank, by_row):
    shape = (columns, rank) if by_row else (rank, columns)
    c = lax.broadcasted_iota(jnp.int32, shape, 0 if by_row else 1)
    r = lax.broadcasted_iota(jnp.int32, shape, 1 if by_row else 0)
    return jnp.where(c % rank == r, 1.0, 0.0).astype(bf16)


def halves(v):
    high = v.astype(bf16)
    return high, (v - high.astype(f32)).astype(bf16)


def dot(a, b, dims=(((1,), (0,)), ((), ()))):
    return lax.dot_general(a, b, dims, preferred_element_type=f32)


def dot2(v, b, dims=(((1,), (0,)), ((), ()))):
    high, low = halves(v)
    return dot(high, b, dims) + dot(low, b, dims)


class Stream:
    def __init__(self, ahead):
        self.moves, self.ahead, self.taken, self.begun = [], ahead, 0, 0

    def add(self, src, dst, sem):
        self.moves.append(pltpu.make_async_copy(src, dst, sem))

    def fill(self):
        while self.begun < min(self.taken + self.ahead, len(self.moves)):
            self.moves[self.begun].start()
            self.begun += 1

    def take(self, count=1):
        for _ in range(count):
            self.fill()
            self.moves[self.taken].wait()
            self.taken += 1
        self.fill()


def pack_kernel(
    index_ref, table_hbm, tokens_hbm, cotangent_hbm, out_ref,
    table_ref, tokens_ref, cotangent_ref, sems,
):
    moves = [
        pltpu.make_async_copy(a, b, sems.at[i])
        for i, (a, b) in enumerate(
            (
                (table_hbm, table_ref),
                (tokens_hbm, tokens_ref),
                (cotangent_hbm, cotangent_ref),
            )
        )
    ]
    for m in moves:
        m.start()
    for m in moves:
        m.wait()
    width = tokens_ref.shape[1]
    slot = table_ref[index_ref[0]]
    lane = lax.broadcasted_iota(jnp.int32, (1, SPLIT), 1)
    digits = jnp.where(lane == 0, slot // SPLIT, jnp.where(lane == 1, slot % SPLIT, 0))
    digits = digits.astype(f32).astype(bf16)
    for i in range(out_ref.shape[0]):
        out_ref[i, 0:1, :width] = tokens_ref[...]
        out_ref[i, 1:2, :width] = cotangent_ref[...]
        out_ref[i, 0:1, width:] = digits
        out_ref[i, 1:2, width:] = digits


def blocks(size, step):
    return [pl.ds(i * step, step) for i in range(size // step)]


def forward_kernel(
    rank, parts,
    x_ref, c_ref, slot_ref, wg_hbm, wu_hbm, wd_hbm, d_hbm, u_hbm,
    gate_ref, up_ref, hid_ref, pay_ref, base_ref, pull_ref, wg_ref, d_ref, u_ref,
    wu_ref, wd_ref, sg, su, sd, sf,
):
    total, width = x_ref.shape
    hidden_dev = wg_ref.shape[1]
    units = hidden_dev // parts
    tall = fit(width, PIECE // units)
    flat = fit(units, PIECE // width)
    stream = Stream(AHEAD)
    stream.add(u_hbm, u_ref, sf.at[0])
    for p, f in enumerate(blocks(hidden_dev, units)):
        for j, k in enumerate(blocks(width, tall)):
            stream.add(wg_hbm.at[k, f], wg_ref.at[k, f], sg.at[p, j])
        for j, k in enumerate(blocks(width, tall)):
            stream.add(wu_hbm.at[k, f], wu_ref.at[k], su.at[p, j])
        if p == parts - 1:
            stream.add(d_hbm, d_ref, sf.at[1])
        for j, k in enumerate(blocks(units, flat)):
            at = pl.ds(p * units + j * flat, flat)
            stream.add(wd_hbm.at[at], wd_ref.at[k], sd.at[p, j])
    stream.fill()
    half = total // 2
    slot = slot_ref[...]

    stream.take()
    kept = u_ref.shape[0]
    first = lax.axis_index("tensor") * (kept // rank)
    pulled = dot(c_ref[...], u_ref[...], NT)
    pulled = jnp.where(slot_mask(slot, first, kept, rank), pulled, 0.0)
    rank_out = adapter_scale * dot2(pulled, fold_matrix(kept, rank, True))

    def project(w_ref, f):
        acc = jnp.zeros((total, units), f32)
        for k in blocks(width, fit(width, 2 * tall)):
            stream.take(k.size // tall)
            acc = acc + dot(x_ref[:, k], w_ref[k, f])
        return acc

    step = fit(width, 2048)
    for p, f in enumerate(blocks(hidden_dev, units)):
        gate = project(wg_ref, f)
        gate_ref[:, f] = gate
        up = project(wu_ref, slice(None))
        up_ref[:, f] = up
        hid = (gate * jax.nn.sigmoid(gate) * up).astype(bf16)
        hid_ref[:, f] = hid
        if p == parts - 1:
            stream.take()
            columns = d_ref.shape[0]
            met = dot(hid_ref[...], d_ref[...], NT)
            met = jnp.where(slot_mask(slot, 0, columns, rank), met, 0.0)
            rank_in = dot2(met, fold_matrix(columns, rank, True))
        stream.take(units // flat)
        pull_ref[:, f] = dot(c_ref[...], wd_ref[...], NT)
        for s in blocks(width, step):
            part = dot(hid, wd_ref[:, s])
            base_ref[:, s] = part if p == 0 else base_ref[:, s] + part

    both = jnp.concatenate((rank_in, rank_out), axis=1)
    swap = lax.axis_index("tensor") % 2
    own, sib = both[:half], both[half:]
    pay = jnp.concatenate(
        (
            jnp.where(swap == 0, own, sib),
            jnp.where(swap == 0, sib, own),
            jnp.zeros((half, pay_ref.shape[2] - 4 * rank), f32),
        ),
        axis=1,
    )
    for i in range(pay_ref.shape[0]):
        pay_ref[i] = pay


def backward_kernel(
    rank,
    got_ref, slot_ref, gate_ref, up_ref, base_ref, pull_ref, wg_ref, wu_hbm, d_ref, u_ref,
    own_ref, sib_ref, left_ref, weighted_ref,
    wu_ref, su,
):
    total, hidden_dev = gate_ref.shape
    width = wg_ref.shape[0]
    piece = fit(width, 1024)
    stream = Stream(2)
    for j, k in enumerate(blocks(width, piece)):
        stream.add(wu_hbm.at[k], wu_ref.at[k], su.at[j])
    stream.fill()
    half = total // 2
    columns = d_ref.shape[0]
    kept = u_ref.shape[0]
    got = jnp.sum(got_ref[...], axis=0)
    swap = lax.axis_index("tensor") % 2
    a, b = got[:, : 2 * rank], got[:, 2 * rank : 4 * rank]
    both = jnp.concatenate(
        (jnp.where(swap == 0, a, b), jnp.where(swap == 0, b, a)), axis=0
    )
    rank_in = both[:, :rank]
    rank_out = both[:, rank:].astype(bf16)
    spread = dot(rank_out, fold_matrix(columns, rank, False))
    slot = slot_ref[...]
    left = jnp.where(slot_mask(slot, 0, columns, rank), spread, 0.0).astype(bf16)
    left_ref[...] = left
    grad = pull_ref[...] + dot(left, d_ref[...])
    gate = gate_ref[...]
    up = up_ref[...]
    sig = jax.nn.sigmoid(gate)
    gg = (grad * up * sig * (1.0 + gate * (1.0 - sig))).astype(bf16)
    gu = (grad * (gate * sig)).astype(bf16)
    first = lax.axis_index("tensor") * (kept // rank)
    mine = slot_mask(slot, first, kept, rank)
    high, low = halves(rank_in)
    fold = fold_matrix(kept, rank, False)
    high = jnp.where(mine, dot(high, fold), 0.0).astype(bf16)
    low = jnp.where(mine, dot(low, fold), 0.0).astype(bf16)
    weighted_ref[...] = jnp.concatenate((high, low), axis=0)
    for s in blocks(width, piece):
        us = u_ref[:, s]
        adapted = adapter_scale * (dot(high, us) + dot(low, us))
        out = base_ref[:, s] + adapted.astype(bf16).astype(f32)
        own_ref[0, :, s] = out[:half]
        sib_ref[0, :, s] = out[half:].astype(bf16)
        stream.take()
        for i in range(4):
            t = pl.ds(s.start + i * piece // 4, piece // 4)
            inp = dot(gg, wg_ref[t, :], NT) + dot(gu, wu_ref[t, :], NT)
            own_ref[1, :, t] = inp[:half]
            sib_ref[1, :, t] = inp[half:].astype(bf16)


def factor_kernel(left_ref, hid_ref, weighted_ref, c_ref, down_ref, upg_ref):
    columns = down_ref.shape[0]
    rows = fit(columns, 256)
    for i in range(columns // rows):
        s = pl.ds(i * rows, rows)
        down_ref[s, :] = dot(left_ref[:, s], hid_ref[...], TN).astype(bf16)
    width = c_ref.shape[1]
    chunk = fit(width, 1024)
    total = c_ref.shape[0]
    for i in range(width // chunk):
        s = pl.ds(i * chunk, chunk)
        cs = c_ref[:, s]
        both = dot(weighted_ref[:total], cs, TN) + dot(weighted_ref[total:], cs, TN)
        upg_ref[:, s] = (adapter_scale * both).astype(bf16)


def combine_kernel(own_ref, got_ref, out_ref):
    for i in range(own_ref.shape[0]):
        both = own_ref[i] + got_ref[i].astype(f32)
        out_ref[:, i, :] = both.astype(bf16)


def finish_kernel(back_ref, mixed_ref, grad_ref):
    total = jnp.sum(back_ref[...].astype(f32), axis=0).astype(bf16)
    rows = mixed_ref.shape[0]
    mixed_ref[...] = total[:rows]
    grad_ref[...] = total[rows:]


def call(kernel, args, outs, mib, specs=None, out_specs=None, flops=0, nbytes=0, scratch=()):
    return pl.pallas_call(
        kernel,
        in_specs=specs or [VMEM] * len(args),
        out_specs=out_specs or [VMEM] * len(outs),
        out_shape=[jax.ShapeDtypeStruct(*o) if isinstance(o, tuple) else o for o in outs],
        scratch_shapes=scratch,
        compiler_params=params(mib),
        cost_estimate=pl.CostEstimate(flops=flops, bytes_accessed=nbytes, transcendentals=0),
    )(*args)


def held(x):
    return pltpu.with_memory_space_constraint(x, pltpu.VMEM)


def far(x):
    return pltpu.with_memory_space_constraint(x, pltpu.HBM)


def per_device(
    tokens,
    cotangent,
    token_adapter_index,
    adapter_storage_slot,
    gate_weight,
    up_weight,
    down_weight,
    adapter_down_factors,
    adapter_up_factors,
):
    devices = lax.axis_size("tensor")
    chips = devices // 2
    tok_dev, width = tokens.shape
    hidden_dev = gate_weight.shape[1]
    kept, rank = adapter_up_factors.shape[:2]
    count = adapter_storage_slot.shape[0]
    half = chips * tok_dev
    total = 2 * half
    room = 4 if total <= 16 else 40
    same_core = [[c + 2 * i for i in range(chips)] for c in range(2)]
    pairs = [(i, i ^ 1) for i in range(devices)]
    parts = PARTS if hidden_dev % (256 * PARTS) == 0 else 1
    units = hidden_dev // parts

    wg, wu, wd = far(gate_weight), far(up_weight), far(down_weight)
    d = far(adapter_down_factors.reshape(count * rank, hidden_dev))
    u = far(adapter_up_factors.reshape(kept * rank, width))
    weight_mib = -(-2 * width * hidden_dev >> 20)

    (sent,) = call(
        pack_kernel,
        (token_adapter_index, far(adapter_storage_slot), far(tokens), far(cotangent)),
        (((chips, 2, width + SPLIT), bf16),),
        room,
        specs=[SMEM] + [HBM] * 3,
        scratch=[
            pltpu.SMEM(adapter_storage_slot.shape, jnp.int32),
            pltpu.VMEM(tokens.shape, bf16),
            pltpu.VMEM(cotangent.shape, bf16),
            pltpu.SemaphoreType.DMA((3,)),
        ],
    )
    own = lax.all_to_all(sent, "tensor", 0, 0, axis_index_groups=same_core, tiled=True)
    sib = lax.ppermute(own, "tensor", pairs)
    gathered = jnp.concatenate((own, sib), axis=0).reshape(total, 2, width + SPLIT)
    x = gathered[:, 0, :width]
    c = gathered[:, 1, :width]
    code = gathered[:, 0, width : width + 2].astype(f32)
    slots = code[:, 0:1] * SPLIT + code[:, 1:2]

    sems = pltpu.SemaphoreType.DMA
    gate, up, hid, pay, base, pull, wg, d, u = call(
        functools.partial(forward_kernel, rank, parts),
        (x, c, slots, wg, wu, wd, d, u),
        (
            ((total, hidden_dev), f32),
            ((total, hidden_dev), f32),
            ((total, hidden_dev), bf16),
            ((devices, half, -(-4 * rank // 128) * 128), f32),
            ((total, width), f32),
            ((total, hidden_dev), f32),
            pltpu.VMEM(wg.shape, bf16),
            pltpu.VMEM(d.shape, bf16),
            pltpu.VMEM(u.shape, bf16),
        ),
        room + 6 + -(-2 * weight_mib // parts),
        specs=[VMEM] * 3 + [HBM] * 5,
        scratch=[
            pltpu.VMEM((width, units), bf16),
            pltpu.VMEM((units, width), bf16),
            sems((parts, width // fit(width, PIECE // units))),
            sems((parts, width // fit(width, PIECE // units))),
            sems((parts, units // fit(units, PIECE // width))),
            sems((2,)),
        ],
    )
    got = lax.all_to_all(pay, "tensor", 0, 0)
    mine, theirs, left, weighted = call(
        functools.partial(backward_kernel, rank),
        (got, slots, gate, up, base, pull, held(wg), wu, held(d), held(u)),
        (
            ((2, half, width), f32),
            ((2, half, width), bf16),
            ((total, count * rank), bf16),
            ((2 * total, kept * rank), bf16),
        ),
        room + 6 + weight_mib,
        specs=[VMEM] * 7 + [HBM, VMEM, VMEM],
        scratch=[pltpu.VMEM(wu.shape, bf16), sems((width // fit(width, 1024),))],
    )
    (summed,) = call(
        combine_kernel,
        (mine, lax.ppermute(theirs, "tensor", pairs)),
        (((half, 2, width), bf16),),
        room,
    )
    back = lax.all_to_all(summed, "tensor", 0, 0, axis_index_groups=same_core, tiled=True)
    down_grad, up_factor_gradient = call(
        factor_kernel,
        (left, hid, weighted, c),
        (((count * rank, hidden_dev), bf16), ((kept * rank, width), bf16)),
        room,
        flops=2 * total * count * rank * hidden_dev,
        nbytes=2 * (count * rank * hidden_dev + kept * rank * width),
    )
    mixed, input_grad = call(
        finish_kernel,
        (back,),
        (((tok_dev, width), bf16), ((tok_dev, width), bf16)),
        room,
    )
    return (
        mixed,
        input_grad,
        down_grad.reshape(count, rank, hidden_dev),
        up_factor_gradient.reshape(kept, rank, width),
    )


def solution(mesh):
    in_specs = (
        P(("parts", "tensor"), None),
        P(("parts", "tensor"), None),
        P(("parts", "tensor")),
        P(),
        P(None, "tensor"),
        P(None, "tensor"),
        P("tensor", None),
        P(None, None, "tensor"),
        P("tensor", None, None),
    )
    out_specs = (
        P(("parts", "tensor"), None),
        P(("parts", "tensor"), None),
        P("parts", None, "tensor"),
        P(("parts", "tensor"), None, None),
    )
    return jax.shard_map(
        per_device, mesh=mesh, in_specs=in_specs, out_specs=out_specs, check_vma=False
    )
```
